256 devices in a mesh: pb: 8 (over y, x_lo), ha: 8 (over z), ka: 4 (over x_hi, core).
Axes of the slice: x: 4 (x_hi: 2, x_lo: 2; x = x_hi * 2 + x_lo), y: 4, z: 8, core: 2. Of those that a mesh axis runs over, the one named last changes fastest.
Arguments:
- main_query: bfloat16 [2048, 128, 192], P('pb', 'ha'), may hold values from -210 to 210
- main_key: bfloat16 [8192, 128, 192], P('ka', 'ha'), may hold values from -6 to 6
- index_query: bfloat16 [2048, 64, 128], P('pb', 'ha'), may hold values from -45 to 45
- index_weight: bfloat16 [2048, 64], P('pb', 'ha'), may hold values from -0.099609375 to 0.29882812
- index_key: bfloat16 [8192, 128], P(('pb', 'ka')), may hold values from -6 to 6
- query_pos: int32 [2048], P('pb'), may hold values from 1 to 8191
Outputs:
- grad_query: float32 [2048, 64, 128], P(('pb', 'ka'), 'ha')
- grad_weight: float32 [2048, 64], P(('pb', 'ka'), 'ha')
- grad_key: float32 [8192, 128], P(('pb', 'ka'))
The draws below stay inside these ranges and needn't reach their ends.
All inputs are finite; a program needn't handle non-finite values.
Results may differ from the reference program's by a relative error of at most 0.00095.
Values may be sent and summed in bfloat16 or wider, within the bound.
A program may use at most 192 MiB of HBM per device.

```python
import math
import jax
import jax.numpy as jnp
from jax import lax

HM = 128
DH = 192
HI = 64
DI = 128
K_DEV = 2048
KBLK = 256
QUERIES = 2048
KEYS = 8192
N_PB = 8
N_KA = 4


def main_base(key):
    return jnp.clip(jax.random.normal(jax.random.fold_in(key, 55), (KEYS, HM, DH), jnp.float32), -6.0, 6.0)


def index_base(key):
    return jnp.clip(jax.random.normal(jax.random.fold_in(key, 77), (KEYS, DI), jnp.float32), -6.0, 6.0)


def draw_main_key(key, part):
    shared = main_base(key)
    return shared.astype(jnp.bfloat16)


def draw_main_query(key, part):
    key = jax.random.fold_in(key, 2)
    values = jnp.clip(jax.random.normal(key, (QUERIES, HM, DH), jnp.float32), -6.0, 6.0)
    return values.astype(jnp.bfloat16)


def draw_index_key(key, part):
    shared = index_base(key)
    stored = shared.reshape(KEYS // K_DEV, K_DEV // KBLK, KBLK, DI).transpose(1, 0, 2, 3).reshape(KEYS, DI)
    return stored.astype(jnp.bfloat16)


def draw_index_query(key, part):
    key = jax.random.fold_in(key, 4)
    values = jnp.clip(jax.random.normal(key, (QUERIES, HI, DI), jnp.float32), -6.0, 6.0)
    return values.astype(jnp.bfloat16)


def plant(entries, own_key, smallest, top_value):
    shape = entries.shape
    spot = [jax.random.randint(jax.random.fold_in(own_key, axis), (), 0, shape[axis]) for axis in range(len(shape))]
    entries = entries.at[tuple(spot)].set(smallest)
    longest = shape.index(max(shape))
    spot[longest] = (spot[longest] + 1) % shape[longest]
    return entries.at[tuple(spot)].set(top_value)


def shard_levels(rng, shape, pieces, low, high):
    def one(dim, shards_of):
        steps = jax.random.uniform(jax.random.fold_in(jax.random.fold_in(rng, 6), dim), (shards_of,), jnp.float32, low / len(pieces), high / len(pieces))
        return jnp.repeat(jnp.exp(steps), shape[dim] // shards_of).reshape((-1,) + (1,) * (len(shape) - dim - 1))

    loudness = one(*pieces[0])
    for cut in pieces[1:]:
        loudness = loudness * one(*cut)
    return loudness


def setup_inputs(seed: int = 0) -> dict:
    keys = jax.random.split(jax.random.key(seed), 7)
    return {
        "main_query": draw_main_query(jax.random.fold_in(keys[6], 71), 0),
        "main_key": draw_main_key(jax.random.fold_in(keys[6], 71), 0),
        "index_query": draw_index_query(jax.random.fold_in(keys[6], 71), 0),
        "index_weight": jnp.clip(-0.099609375 + 0.3984375 * jax.random.uniform(keys[3], (QUERIES, HI), jnp.float32) ** shard_levels(keys[3], (QUERIES, HI), ((0, 8), (1, 8)), -0.2, 0.2), -0.099609375, 0.29882812).astype(jnp.bfloat16),
        "index_key": draw_index_key(jax.random.fold_in(keys[6], 71), 0),
        "query_pos": plant(jax.random.randint(keys[5], (QUERIES,), 1, KEYS), jax.random.fold_in(keys[5], 1), 1, KEYS - 1).astype(jnp.int32),
    }


def reference(main_query, main_key, index_query, index_weight, index_key, query_pos):
    ctx_key = index_key.reshape(N_PB, N_KA, KBLK, DI).transpose(1, 0, 2, 3).reshape(KEYS, DI)
    ctx_wide = ctx_key.astype(jnp.float32)
    visible = jnp.arange(KEYS, dtype=jnp.int32)[None, :] <= query_pos[:, None]
    scale = 1.0 / math.sqrt(DI)

    def main_head(total, pair):
        query_rows, key_rows = pair
        scores = jnp.dot(query_rows, key_rows.T, preferred_element_type=jnp.float32) / math.sqrt(DH)
        scores = jnp.where(visible, scores, -jnp.inf)
        return (total + jax.nn.softmax(scores, axis=1), None)
    summed, unused = lax.scan(main_head, jnp.zeros((QUERIES, KEYS), jnp.float32), (main_query.transpose(1, 0, 2), main_key.transpose(1, 0, 2)))
    target = summed / HM

    def index_head(total, pair):
        query_rows, weights = pair
        acts = jnp.dot(query_rows, ctx_key.T, preferred_element_type=jnp.float32) * scale
        return (total + weights.astype(jnp.float32)[:, None] * jnp.maximum(acts, 0.0), None)
    logits, unused = lax.scan(index_head, jnp.zeros((QUERIES, KEYS), jnp.float32), (index_query.transpose(1, 0, 2), index_weight.T))
    prob = jax.nn.softmax(jnp.where(visible, logits, -jnp.inf), axis=1)
    diff = (prob - target) * (KEYS / 16.0)

    def back_head(total, pair):
        query_rows, weights = pair
        acts = jnp.dot(query_rows, ctx_key.T, preferred_element_type=jnp.float32) * scale
        relu_act = jnp.maximum(acts, 0.0)
        weight_grad = lax.optimization_barrier(jnp.sum(diff * relu_act, axis=1))
        gate = jnp.where(acts > 0, diff * weights.astype(jnp.float32)[:, None], 0.0)
        query_grad = jnp.dot(gate, ctx_wide, precision=lax.Precision.HIGHEST) * scale
        total = total + jnp.dot(gate.T, query_rows.astype(jnp.float32), precision=lax.Precision.HIGHEST) * scale
        return (total, (query_grad, weight_grad))
    ctx_grad, (query_grads, weight_grads) = lax.scan(back_head, jnp.zeros((KEYS, DI), jnp.float32), (index_query.transpose(1, 0, 2), index_weight.T))
    grad_query = query_grads.transpose(1, 0, 2)
    grad_weight = weight_grads.T
    grad_key = ctx_grad.reshape(N_KA, N_PB, KBLK, DI).transpose(1, 0, 2, 3).reshape(KEYS, DI)
    return (grad_query, grad_weight, grad_key)
```

```python
import functools
import math

import jax
import jax.numpy as jnp
from jax import lax
from jax.experimental import pallas as pl
from jax.experimental.pallas import tpu as pltpu
from jax.sharding import PartitionSpec as P

MESH = pl.DeviceIdType.MESH
LOW = -1e30
LANES = 128
NBUF = 4
EXTRA = 6
LOG2E = 1.4426950408889634


def lane_spread(row):
    return jnp.transpose(jnp.broadcast_to(row, (LANES, LANES)), (1, 0))


def kernel(
    dims,
    q_ref, kt_ref, pos_ref, iq_ref, wc_ref, wn_ref, ik_ref,
    gq_ref, gw_ref, gk_ref,
    kbuf, s0, s1, e_ref, f_ref, stm, stl, st_tx, st_rx, comb,
    t_ref, rxa, rxb,
    iq_all, wc_all, w_rep, wq_t, ctx, ctx_t, m_ref, lg, d_hi, d_lo,
    ix_tx, ix_rx,
    u_ref, u_rx, v_ref, v_rx, r_ref, o_rx,
    gk_tx, gk_rx, z_tx, z_rx, zsum,
    ksem, st_s, st_r, ra_s, ra_r, rb_s, rb_r, iq_s, iq_r, wc_s, wc_r, cx_s, cx_r,
    ix_s, ix_r, u_s, u_r, v_s, v_r, o_s, o_r, gk_s, gk_r, z_s, z_r, y_s, y_r,
):
    n_pb, n_ha, n_ka, heads, dh, keys, main_total, key_total = dims
    p, h, k = lax.axis_index("pb"), lax.axis_index("ha"), lax.axis_index("ka")
    half = n_ha // 2
    rows = half * 32
    groups = rows // 8
    tiles = keys // LANES
    slots = heads + EXTRA
    scale_main = LOG2E / math.sqrt(dh)
    scale = 1.0 / math.sqrt(128)

    offsets = [half]
    for o in range(half - 1, 0, -1):
        offsets += [-o, o]
    offsets += [0]

    def copy_to(src, dst, ss, rs, dev):
        return pltpu.make_async_remote_copy(
            src_ref=src, dst_ref=dst, send_sem=ss, recv_sem=rs, device_id=dev, device_id_type=MESH
        )

    def pb_dev(i):
        return {"pb": lax.rem(p + i, n_pb)}

    def ha_dev(i):
        return {"ha": lax.rem(h + i + n_ha, n_ha)}

    def ka_dev(i):
        return {"ka": lax.rem(k + i, n_ka)}

    def kcopy(head, slot):
        return pltpu.make_async_copy(kt_ref.at[head], kbuf.at[slot], ksem.at[slot])

    for n in range(NBUF):
        kcopy(n, n).start()

    barrier = pltpu.get_barrier_semaphore()
    for i in range(1, n_ha):
        pl.semaphore_signal(barrier, inc=1, device_id=ha_dev(i), device_id_type=MESH)
    for i in range(1, n_pb):
        pl.semaphore_signal(barrier, inc=1, device_id=pb_dev(i), device_id_type=MESH)
    for i in range(1, n_ka):
        pl.semaphore_signal(barrier, inc=1, device_id=ka_dev(i), device_id_type=MESH)
    pl.semaphore_wait(barrier, n_ha + n_pb + n_ka - 3)

    def iq_copy(i):
        dest = lax.rem(h + i, n_ha)
        return copy_to(
            iq_ref.at[:, pl.ds(pl.multiple_of(dest * 64, 64), 64), :],
            iq_all.at[:, pl.ds(pl.multiple_of(h * 64, 64), 64), :],
            iq_s.at[i], iq_r.at[i], ha_dev(i),
        )

    def wc_copy(i):
        dest = lax.rem(h + i, n_ha)
        return copy_to(wc_ref.at[dest], wc_all.at[h], wc_s.at[i], wc_r.at[i], ha_dev(i))

    def cx_copy(i):
        return copy_to(
            ik_ref, ctx.at[pl.ds(pl.multiple_of(p * 256, 256), 256), :], cx_s.at[i], cx_r.at[i], pb_dev(i)
        )

    for i in range(1, n_pb):
        cx_copy(i).start()
    for i in range(1, n_ha):
        iq_copy(i).start()
        wc_copy(i).start()

    lane = lax.broadcasted_iota(jnp.int32, (8, LANES), 1)
    lane_rows = lax.broadcasted_iota(jnp.int32, (rows, LANES), 1)
    first_key = k * keys

    def dest_of(i):
        return lax.rem(h + offsets[i] + n_ha, n_ha)

    def scores(st, head, slot, out):
        q = jnp.concatenate([q_ref[head, dest_of(st * half + i)] for i in range(half)], axis=0)
        out[...] = jnp.dot(q, kbuf[slot], preferred_element_type=jnp.float32)

    def eslot(st, head):
        return lax.rem(st * heads + head, slots) if not isinstance(head, int) else (st * heads + head) % slots

    def soften(st, head, src):
        slot = eslot(st, head)
        tops, sums = [], []
        for g in range(groups):
            rel = pos_ref[dest_of(st * half + g // 4), pl.ds((g % 4) * 8, 8), :] - first_key - lane
            x = [
                jnp.where(rel >= c * LANES, src[g * 8 : g * 8 + 8, c * LANES : (c + 1) * LANES], LOW)
                for c in range(tiles)
            ]
            top = functools.reduce(jnp.maximum, x)
            total = None
            for c in range(tiles):
                e = jnp.exp2((x[c] - top) * scale_main)
                e_ref[slot, g * 8 : g * 8 + 8, c * LANES : (c + 1) * LANES] = e
                total = e if total is None else total + e
            tops.append(top)
            sums.append(total)
        tops = jnp.concatenate(tops, axis=0)
        sums = jnp.concatenate(sums, axis=0)
        f_ref[st, head] = tops
        row_top = jnp.max(tops, axis=1, keepdims=True)
        row_sum = jnp.sum(sums * jnp.exp2((tops - row_top) * scale_main), axis=1, keepdims=True)
        stm[...] = jnp.where(lane_rows == head, row_top, stm[...])
        stl[...] = jnp.where(lane_rows == head, row_sum, stl[...])

    def st_copy(st, i):
        return copy_to(st_tx.at[st], st_rx.at[st, i], st_s.at[st, i], st_r.at[st, i], ka_dev(i))

    def send_stats(st):
        st_tx[st, 0:heads] = jnp.transpose(stm[...], (1, 0))[0:heads]
        st_tx[st, heads : 2 * heads] = jnp.transpose(stl[...], (1, 0))[0:heads]
        for i in range(1, n_ka):
            st_copy(st, i).start()

    def finish(st):
        for i in range(1, n_ka):
            st_copy(st, i).wait_recv()
        tops = [st_tx[st, 0:heads]] + [st_rx[st, i, 0:heads] for i in range(1, n_ka)]
        sums = [st_tx[st, heads : 2 * heads]] + [st_rx[st, i, heads : 2 * heads] for i in range(1, n_ka)]
        top = functools.reduce(jnp.maximum, tops)
        total = functools.reduce(
            jnp.add, [b * jnp.exp2((a - top) * scale_main) for a, b in zip(tops, sums)]
        )
        comb[0:heads] = top
        comb[heads : 2 * heads] = 1.0 / (total * main_total)
        cols = jnp.transpose(comb[...], (1, 0))
        for head in range(heads):
            gtop = jnp.broadcast_to(cols[:, head : head + 1], (rows, LANES))
            ginv = jnp.broadcast_to(cols[:, heads + head : heads + head + 1], (rows, LANES))
            f_ref[st, head] = jnp.exp2((f_ref[st, head] - gtop) * scale_main) * ginv

        def one(g, carry):
            at = pl.ds(pl.multiple_of(g * 8, 8), 8)
            acc = [jnp.zeros((8, LANES), jnp.float32) for _ in range(tiles)]
            for head in range(heads):
                f = f_ref[st, head, at, :]
                slot = eslot(st, head)
                for c in range(tiles):
                    acc[c] = acc[c] + f * e_ref[slot, at, c * LANES : (c + 1) * LANES]
            spot = st * half + g // 4
            to = pl.ds(pl.multiple_of(lax.rem(g, 4) * 8, 8), 8)
            for c in range(tiles):
                part, inner = divmod(c, tiles // 2)
                t_ref[spot, part, to, inner * LANES : (inner + 1) * LANES] = acc[c]
            return carry

        lax.fori_loop(0, groups, one, 0)

    def spot_of(offset):
        return offsets.index(offset)

    def ra_copy(a, c):
        src = t_ref.at[spot_of(half if a == 0 else -(half - a)), c]
        return copy_to(src, rxa.at[a, c], ra_s.at[a, c], ra_r.at[a, c], ha_dev(-1))

    def rb_copy(a, c):
        src = t_ref.at[spot_of(half - a), c]
        return copy_to(src, rxb.at[a, c], rb_s.at[a, c], rb_r.at[a, c], ha_dev(1))

    def chain_a(a, c):
        if a > 1 or (a == 1 and c == 0):
            ra_copy(a - 1, c).wait_recv()
            spot = spot_of(-(half - a))
            t_ref[spot, c] = t_ref[spot, c] + rxa[a - 1, c]
        ra_copy(a, c).start()

    def chain_b(a, c):
        if a > 1 or (a == 1 and c == 1):
            rb_copy(a - 1, c).wait_recv()
            spot = spot_of(half - a)
            t_ref[spot, c] = t_ref[spot, c] + rxb[a - 1, c]
        rb_copy(a, c).start()

    def fwd(st, after):
        last = st == 1
        kcopy(0, 0).wait()
        scores(st, 0, 0, s0)
        kcopy(NBUF, 0).start()

        def pair(i, carry):
            h0 = 2 * i
            a = lax.rem(h0 + 1, NBUF)
            b = lax.rem(h0 + 2, NBUF)
            kcopy(h0 + 1, a).wait()
            kcopy(h0 + 2, b).wait()
            scores(st, h0 + 1, a, s1)
            soften(st, h0, s0)
            scores(st, h0 + 2, b, s0)
            soften(st, h0 + 1, s1)

            def refill():
                kcopy(lax.rem(h0 + 1 + NBUF, heads), a).start()
                kcopy(lax.rem(h0 + 2 + NBUF, heads), b).start()

            if last:
                pl.when(h0 + 1 + NBUF < heads)(lambda: kcopy(h0 + 1 + NBUF, a).start())
                pl.when(h0 + 2 + NBUF < heads)(lambda: kcopy(h0 + 2 + NBUF, b).start())
            else:
                refill()
            after(i)
            return carry

        lax.fori_loop(0, heads // 2 - 1, pair, 0)
        end = (heads - 1) % NBUF
        kcopy(heads - 1, end).wait()
        scores(st, heads - 1, end, s1)
        if not last:
            kcopy(NBUF - 1, end).start()
        soften(st, heads - 2, s0)
        soften(st, heads - 1, s1)

    fwd(0, lambda i: None)
    send_stats(0)

    def beside(i):
        @pl.when(i == EXTRA // 2 - 1)
        def _():
            finish(0)
            chain_a(0, 0)
            chain_b(0, 1)
            chain_a(1, 1)
            chain_b(1, 0)

        @pl.when(i == EXTRA // 2 + 1)
        def _():
            chain_a(1, 0)
            chain_b(1, 1)

        @pl.when(i == EXTRA // 2 + 3)
        def _():
            chain_a(2, 1)
            chain_a(2, 0)

    fwd(1, beside)
    send_stats(1)

    iq_all[:, pl.ds(pl.multiple_of(h * 64, 64), 64), :] = iq_ref[:, pl.ds(pl.multiple_of(h * 64, 64), 64), :]
    wc_all[h] = wc_ref[h]
    ctx[pl.ds(pl.multiple_of(p * 256, 256), 256), :] = ik_ref[...]
    for i in range(1, n_pb):
        cx_copy(i).wait_recv()
    for i in range(1, n_ha):
        iq_copy(i).wait_recv()
        wc_copy(i).wait_recv()
    ctx_t[...] = jnp.transpose(ctx[...].astype(jnp.float32), (1, 0)).astype(jnp.bfloat16)
    for src in range(n_ha):
        for kk in range(n_ka // 2):
            spread = lane_spread(wc_all[src, kk : kk + 1, :])
            for one in range(2):
                w_rep[2 * kk + one, src * 64 : src * 64 + 64, :] = spread[one * 64 : one * 64 + 64]
    per = n_ha * 64
    for kk in range(n_ka):
        wq = jnp.transpose(w_rep[kk] * iq_all[kk].astype(jnp.float32), (1, 0))
        big = wq.astype(jnp.bfloat16)
        wq_t[0:128, kk * per : (kk + 1) * per] = big
        wq_t[128:256, kk * per : (kk + 1) * per] = (wq - big.astype(jnp.float32)).astype(jnp.bfloat16)

    finish(1)
    for c in range(2):
        chain_b(2, c)

    step = 512

    def index_part(n, carry):
        kk, sc = n // (keys // step), lax.rem(n, keys // step)
        at = pl.ds(pl.multiple_of(sc * step, step), step)
        act = jnp.dot(iq_all[kk], ctx_t[:, at], preferred_element_type=jnp.float32)
        w = w_rep[kk]
        parts = []
        for c in range(step // LANES):
            a = act[:, c * LANES : (c + 1) * LANES]
            r = jnp.maximum(a, 0.0) * w
            parts.append(jnp.sum(jnp.sum(r.reshape(n_ha, 64, LANES), axis=0).reshape(8, 8, LANES), axis=1))
        lg[kk, :, at] = jnp.concatenate(parts, axis=1) * scale
        m_ref[kk, :, at] = jnp.where(act > 0, 1.0, 0.0).astype(jnp.bfloat16)
        return carry

    total_parts = n_ka * (keys // step)
    lax.fori_loop(0, total_parts // 2, index_part, 0)
    for c in range(2):
        chain_a(3, c)
        chain_b(3, c)
    lax.fori_loop(total_parts // 2, total_parts, index_part, 0)

    me = dest_of(n_ha - 1)
    rel = pos_ref[me][:, 0:1] - first_key
    seen = lax.broadcasted_iota(jnp.int32, (32, keys), 1) <= rel
    logits = jnp.where(seen, lg[...].reshape(32, keys), LOW)
    row_top = jnp.max(logits, axis=1, keepdims=True)
    expo = jnp.where(seen, jnp.exp(logits - row_top), 0.0)
    row_sum = jnp.sum(expo, axis=1, keepdims=True)
    lg[...] = expo.reshape(n_ka, 8, keys)
    ix_tx[0] = jnp.broadcast_to(row_top, (32, LANES))
    ix_tx[1] = jnp.broadcast_to(row_sum, (32, LANES))

    def ix_copy(i):
        return copy_to(ix_tx, ix_rx.at[i], ix_s.at[i], ix_r.at[i], ka_dev(i))

    for i in range(1, n_ka):
        ix_copy(i).start()
    for i in range(1, n_ka):
        ix_copy(i).wait_recv()
    tops = [ix_tx[0]] + [ix_rx[i, 0] for i in range(1, n_ka)]
    sums = [ix_tx[1]] + [ix_rx[i, 1] for i in range(1, n_ka)]
    top = functools.reduce(jnp.maximum, tops)
    total = functools.reduce(jnp.add, [b * jnp.exp(a - top) for a, b in zip(tops, sums)])
    factor = (jnp.exp(tops[0] - top) / total)[:, 0:1]

    for c in range(2):
        ra_copy(half - 1, c).wait_recv()
        rb_copy(half - 1, c).wait_recv()
        at = slice(c * (keys // 2), (c + 1) * (keys // 2))
        target = t_ref[n_ha - 1, c] + rxa[half - 1, c] + rxb[half - 1, c]
        diff = (lg[:, :, at].reshape(32, keys // 2) * factor - target) * (key_total / 16.0)
        big = diff.astype(jnp.bfloat16).astype(jnp.float32)
        small = diff - big
        for t in range(32):
            kk, r = divmod(t, 8)
            if r % 2:
                continue
            for value, ref in ((big, d_hi), (small, d_lo)):
                both = jnp.concatenate(
                    [
                        jnp.broadcast_to(value[t : t + 1], (8, keys // 2)),
                        jnp.broadcast_to(value[t + 1 : t + 2], (8, keys // 2)),
                    ],
                    axis=0,
                )
                ref[kk, r * 8 : r * 8 + 16, at] = both.astype(jnp.bfloat16)

    u_ref[...] = jnp.zeros_like(u_ref)

    def gk_copy(i):
        return copy_to(gk_tx.at[i], gk_rx.at[i], gk_s.at[i], gk_r.at[i], pb_dev(i))

    def back(n, carry):
        i = n + 1
        dest = lax.rem(p + i, n_pb)
        at = pl.ds(pl.multiple_of(dest * 256, 256), 256)
        key = ctx[at, :]
        wide = jnp.zeros((256, 256), jnp.float32)
        thin = jnp.zeros((128, 256), jnp.float32)
        for kk in range(n_ka):
            mask = m_ref[kk, :, at].reshape(n_ha, 64, 256)
            hi = (mask * d_hi[kk, :, at][None]).reshape(per, 256)
            lo = (mask * d_lo[kk, :, at][None]).reshape(per, 256)
            u_ref[kk] = u_ref[kk] + (
                jnp.dot(hi, key, preferred_element_type=jnp.float32)
                + jnp.dot(lo, key, preferred_element_type=jnp.float32)
            )
            wide += jnp.dot(wq_t[:, kk * per : (kk + 1) * per], hi, preferred_element_type=jnp.float32)
            thin += jnp.dot(wq_t[0:128, kk * per : (kk + 1) * per], lo, preferred_element_type=jnp.float32)
        block = (wide[0:128] + wide[128:256] + thin) * scale
        gk_tx[lax.rem(i, n_pb)] = jnp.transpose(block, (1, 0))

        @pl.when(i < n_pb)
        def _():
            gk_copy(i).start()

        return carry

    lax.fori_loop(0, n_pb, back, 0)

    core, far = lax.rem(k, 2), k // 2

    def u_copy(x):
        return copy_to(
            u_ref.at[x * 2 + 1 - core], u_rx.at[x], u_s.at[x], u_r.at[x], {"ka": far * 2 + 1 - core}
        )

    for x in range(2):
        u_copy(x).start()
    for x in range(2):
        u_copy(x).wait_recv()
        v_ref[x] = u_ref[x * 2 + core] + u_rx[x]
    v_copy = copy_to(v_ref.at[1 - far], v_rx, v_s.at[0], v_r.at[0], {"ka": (1 - far) * 2 + core})
    v_copy.start()

    own = gk_tx[0]
    for i in range(1, n_pb):
        gk_copy(i).wait_recv()
        own = own + gk_rx[i]
    z_tx[...] = own.reshape(n_ha, 256 // n_ha, 128)

    def z_copy(i):
        return copy_to(z_tx.at[lax.rem(h + i, n_ha)], z_rx.at[i], z_s.at[i], z_r.at[i], ha_dev(i))

    for i in range(1, n_ha):
        z_copy(i).start()

    v_copy.wait_recv()
    r_ref[...] = (v_ref[far] + v_rx[...]) * scale

    def o_copy(i):
        dest = lax.rem(h + i, n_ha)
        return copy_to(
            r_ref.at[pl.ds(pl.multiple_of(dest * 64, 64), 64), :], o_rx.at[h], o_s.at[i], o_r.at[i], ha_dev(i)
        )

    for i in range(1, n_ha):
        o_copy(i).start()

    mine = z_tx[h]
    for i in range(1, n_ha):
        z_copy(i).wait_recv()
        mine = mine + z_rx[i]
    zsum[h] = mine

    def y_copy(i):
        return copy_to(zsum.at[h], zsum.at[h], y_s.at[i], y_r.at[i], ha_dev(i))

    for i in range(1, n_ha):
        y_copy(i).start()

    o_rx[h] = r_ref[pl.ds(pl.multiple_of(h * 64, 64), 64), :]
    for i in range(1, n_ha):
        o_copy(i).wait_recv()
    own_rows = pl.ds(pl.multiple_of(k * 4, 4), 4)
    per_row = wn_ref[own_rows, :]
    for b in range(4):
        at = slice(b * LANES, (b + 1) * LANES)
        u = o_rx[2 * b : 2 * b + 2].reshape(LANES, 128)
        gq_ref[at, :] = u * lane_spread(per_row[b : b + 1])
        dots = jnp.transpose(u * iq_ref[k, at, :].astype(jnp.float32), (1, 0))
        gw_ref[:, at] = jnp.broadcast_to(jnp.sum(dots, axis=0, keepdims=True), (8, LANES))

    for i in range(1, n_ha):
        y_copy(i).wait_recv()
    gk_ref[...] = zsum[...].reshape(256, 128)

    for i in range(1, n_pb):
        cx_copy(i).wait_send()
        gk_copy(i).wait_send()
    for i in range(1, n_ha):
        iq_copy(i).wait_send()
        wc_copy(i).wait_send()
        z_copy(i).wait_send()
        o_copy(i).wait_send()
        y_copy(i).wait_send()
    for i in range(1, n_ka):
        for st in range(2):
            st_copy(st, i).wait_send()
        ix_copy(i).wait_send()
    for a in range(half):
        for c in range(2):
            if a or c == 0:
                ra_copy(a, c).wait_send()
            if a or c == 1:
                rb_copy(a, c).wait_send()
    for x in range(2):
        u_copy(x).wait_send()
    v_copy.wait_send()


def body(sizes, main_query, main_key, index_query, index_weight, index_key, query_pos):
    n_pb, n_ha, n_ka = sizes
    t, heads, dh = main_query.shape
    keys = main_key.shape[0]
    joined = index_query.shape[1]
    dims = (n_pb, n_ha, n_ka, heads, dh, keys, heads * n_ha, keys * n_ka)
    q = main_query.reshape(n_ka, n_ha, 8, heads, dh).transpose(3, 1, 0, 2, 4).reshape(heads, n_ha, 32, dh)
    kt = main_key.transpose(1, 2, 0)
    pos = query_pos.reshape(n_ka, n_ha, 8).transpose(1, 0, 2).reshape(n_ha, 32, 1)
    pos = jnp.broadcast_to(pos, (n_ha, 32, LANES))
    iq = index_query.reshape(n_ka, n_ha * 64, 128)
    wide = index_weight.astype(jnp.float32)
    wc = wide.reshape(n_ka, n_ha, 64).transpose(1, 0, 2).reshape(n_ha, n_ka * 64 // LANES, LANES)
    wc = jnp.pad(wc, ((0, 0), (0, 8 - wc.shape[1]), (0, 0)))
    wn = wide.reshape(t * joined // LANES, LANES)

    half = n_ha // 2
    rows = half * 32
    per = n_ha * 64
    f32, bf16 = jnp.float32, jnp.bfloat16
    scratch = [
        pltpu.VMEM((NBUF, dh, keys), bf16),
        pltpu.VMEM((rows, keys), f32),
        pltpu.VMEM((rows, keys), f32),
        pltpu.VMEM((heads + EXTRA, rows, keys), f32),
        pltpu.VMEM((2, heads, rows, LANES), f32),
        pltpu.VMEM((rows, LANES), f32),
        pltpu.VMEM((rows, LANES), f32),
        pltpu.VMEM((2, 2 * heads, rows), f32),
        pltpu.VMEM((2, n_ka, 2 * heads, rows), f32),
        pltpu.VMEM((LANES, rows), f32),
        pltpu.VMEM((n_ha, 2, 32, keys // 2), f32),
        pltpu.VMEM((half, 2, 32, keys // 2), f32),
        pltpu.VMEM((half, 2, 32, keys // 2), f32),
        pltpu.VMEM((n_ka, per, 128), bf16),
        pltpu.VMEM((n_ha, 8, LANES), f32),
        pltpu.VMEM((n_ka, per, LANES), f32),
        pltpu.VMEM((256, n_ka * per), bf16),
        pltpu.VMEM((keys, 128), bf16),
        pltpu.VMEM((128, keys), bf16),
        pltpu.VMEM((n_ka, per, keys), bf16),
        pltpu.VMEM((n_ka, 8, keys), f32),
        pltpu.VMEM((n_ka, 64, keys), bf16),
        pltpu.VMEM((n_ka, 64, keys), bf16),
        pltpu.VMEM((2, 32, LANES), f32),
        pltpu.VMEM((n_ka, 2, 32, LANES), f32),
        pltpu.VMEM((n_ka, per, 128), f32),
        pltpu.VMEM((2, per, 128), f32),
        pltpu.VMEM((2, per, 128), f32),
        pltpu.VMEM((per, 128), f32),
        pltpu.VMEM((per, 128), f32),
        pltpu.VMEM((n_ha, 64, 128), f32),
        pltpu.VMEM((n_pb, 256, 128), f32),
        pltpu.VMEM((n_pb, 256, 128), f32),
        pltpu.VMEM((n_ha, 256 // n_ha, 128), f32),
        pltpu.VMEM((n_ha, 256 // n_ha, 128), f32),
        pltpu.VMEM((n_ha, 256 // n_ha, 128), f32),
    ]
    dma = pltpu.SemaphoreType.DMA
    sems = [dma((NBUF,))]
    for shape in (
        (2, n_ka), (half, 2), (half, 2), (n_ha,), (n_ha,), (n_pb,),
        (n_ka,), (2,), (1,), (n_ha,), (n_pb,), (n_ha,), (n_ha,),
    ):
        sems += [dma(shape), dma(shape)]
    vmem = pl.BlockSpec(memory_space=pltpu.VMEM)
    gq, gw, gk = pl.pallas_call(
        functools.partial(kernel, dims),
        out_shape=(
            jax.ShapeDtypeStruct((per, 128), f32),
            jax.ShapeDtypeStruct((8, per), f32),
            jax.ShapeDtypeStruct((256, 128), f32),
        ),
        in_specs=[vmem, pl.BlockSpec(memory_space=pl.ANY)] + [vmem] * 5,
        out_specs=(vmem, vmem, vmem),
        scratch_shapes=scratch + sems,
        compiler_params=pltpu.CompilerParams(
            collective_id=0, has_side_effects=True, vmem_limit_bytes=63 * 1024 * 1024
        ),
    )(q, kt, pos, iq, wc, wn, index_key)
    return (gq.reshape(t // n_ka, joined, 128), gw[0].reshape(t // n_ka, joined), gk)


def solution(mesh):
    placed = (
        P("pb", "ha", None),
        P("ka", "ha", None),
        P("pb", "ha", None),
        P("pb", "ha"),
        P(("pb", "ka"), None),
        P("pb"),
    )
    sizes = tuple(mesh.shape[name] for name in ("pb", "ha", "ka"))
    return jax.shard_map(
        functools.partial(body, sizes),
        mesh=mesh,
        in_specs=placed,
        out_specs=(P(("pb", "ka"), "ha", None), P(("pb", "ka"), "ha"), P(("pb", "ka"), None)),
        check_vma=False,
    )
```

```python
import functools
import math

import jax
import jax.numpy as jnp
from jax import lax
from jax.experimental import pallas as pl
from jax.experimental.pallas import tpu as pltpu
from jax.sharding import PartitionSpec as P

MESH = pl.DeviceIdType.MESH
LOW = -1e30
LANES = 128
NBUF = 4
EXTRA = 6
LOG2E = 1.4426950408889634


def lane_spread(row):
    return jnp.transpose(jnp.broadcast_to(row, (LANES, LANES)), (1, 0))


def kernel(
    dims,
    qt_ref, kt_ref, iq_ref, wc_ref, ik_ref,
    gq_ref, gw_ref, gk_ref,
    q_ref, q_wide, pos_ref, w_own, kbuf, s0, s1, e_ref, f_ref, stm, stl, st_tx, st_rx, comb,
    t_ref, rxa, rxb,
    iq_all, wc_all, w_rep, wq_t, ctx, ctx_t, m_ref, lg, d_hi, d_lo,
    ix_tx, ix_rx,
    u_ref, u_rx, v_ref, v_rx, r_ref, o_rx,
    gk_tx, gk_rx, z_tx, z_rx, zsum,
    ksem, st_s, st_r, ra_s, ra_r, rb_s, rb_r, iq_s, iq_r, wc_s, wc_r, cx_s, cx_r,
    ix_s, ix_r, u_s, u_r, v_s, v_r, o_s, o_r, gk_s, gk_r, z_s, z_r, y_s, y_r,
):
    n_pb, n_ha, n_ka, heads, dh, keys, main_total, key_total = dims
    p, h, k = lax.axis_index("pb"), lax.axis_index("ha"), lax.axis_index("ka")
    half = n_ha // 2
    rows = half * 32
    groups = rows // 8
    tiles = keys // LANES
    slots = heads + EXTRA
    scale_main = LOG2E / math.sqrt(dh)
    scale = 1.0 / math.sqrt(128)

    offsets = [half]
    for o in range(half - 1, 0, -1):
        offsets += [-o, o]
    offsets += [0]

    def copy_to(src, dst, ss, rs, dev):
        return pltpu.make_async_remote_copy(
            src_ref=src, dst_ref=dst, send_sem=ss, recv_sem=rs, device_id=dev, device_id_type=MESH
        )

    def pb_dev(i):
        return {"pb": lax.rem(p + i, n_pb)}

    def ha_dev(i):
        return {"ha": lax.rem(h + i + n_ha, n_ha)}

    def ka_dev(i):
        return {"ka": lax.rem(k + i, n_ka)}

    def kcopy(head, slot):
        return pltpu.make_async_copy(kt_ref.at[head], kbuf.at[slot], ksem.at[slot])

    for n in range(NBUF):
        kcopy(n, n).start()

    barrier = pltpu.get_barrier_semaphore()
    for i in range(1, n_ha):
        pl.semaphore_signal(barrier, inc=1, device_id=ha_dev(i), device_id_type=MESH)
    for i in range(1, n_pb):
        pl.semaphore_signal(barrier, inc=1, device_id=pb_dev(i), device_id_type=MESH)
    for i in range(1, n_ka):
        pl.semaphore_signal(barrier, inc=1, device_id=ka_dev(i), device_id_type=MESH)
    def iq_copy(i):
        dest = lax.rem(h + i, n_ha)
        return copy_to(
            iq_ref.at[:, pl.ds(pl.multiple_of(dest * 64, 64), 64), :],
            iq_all.at[:, pl.ds(pl.multiple_of(h * 64, 64), 64), :],
            iq_s.at[i], iq_r.at[i], ha_dev(i),
        )

    def wc_copy(i):
        dest = lax.rem(h + i, n_ha)
        return copy_to(wc_ref.at[dest], wc_all.at[h], wc_s.at[i], wc_r.at[i], ha_dev(i))

    def cx_copy(i):
        return copy_to(
            ik_ref, ctx.at[pl.ds(pl.multiple_of(p * 256, 256), 256), :], cx_s.at[i], cx_r.at[i], pb_dev(i)
        )

    def greet():
        pl.semaphore_wait(barrier, n_ha + n_pb + n_ka - 3)
        for i in range(1, n_pb):
            cx_copy(i).start()
        for i in range(1, n_ha):
            iq_copy(i).start()
            wc_copy(i).start()

    lane = lax.broadcasted_iota(jnp.int32, (8, LANES), 1)
    lane_rows = lax.broadcasted_iota(jnp.int32, (rows, LANES), 1)
    first_key = k * keys

    def dest_of(i):
        return lax.rem(h + offsets[i] + n_ha, n_ha)

    for i in range(n_ha):
        pos_ref[i] = lane_spread(wc_ref[dest_of(i), 2:3, :])[0:32].astype(jnp.int32)

    def order_queries(head, carry):
        q_wide[...] = jnp.transpose(qt_ref[head].astype(jnp.float32), (1, 0))
        for i in range(n_ha):
            chunk = [
                q_wide[pl.ds(pl.multiple_of(kk * n_ha * 8 + dest_of(i) * 8, 8), 8), :] for kk in range(n_ka)
            ]
            q_ref[head, i * 32 : i * 32 + 32, :] = jnp.concatenate(chunk, axis=0).astype(jnp.bfloat16)
        return carry

    lax.fori_loop(0, heads, order_queries, 0)

    def scores(st, head, slot, out):
        q = q_ref[head, st * rows : (st + 1) * rows, :]
        out[...] = jnp.dot(q, kbuf[slot], preferred_element_type=jnp.float32)

    def eslot(st, head):
        return lax.rem(st * heads + head, slots) if not isinstance(head, int) else (st * heads + head) % slots

    def soften(st, head, src):
        slot = eslot(st, head)
        tops, sums = [], []
        for g in range(groups):
            rel = pos_ref[st * half + g // 4, (g % 4) * 8 : (g % 4) * 8 + 8, :] - first_key - lane
            x = [
                jnp.where(rel >= c * LANES, src[g * 8 : g * 8 + 8, c * LANES : (c + 1) * LANES], LOW)
                for c in range(tiles)
            ]
            top = functools.reduce(jnp.maximum, x)
            total = None
            for c in range(tiles):
                e = jnp.exp2((x[c] - top) * scale_main)
                e_ref[slot, g * 8 : g * 8 + 8, c * LANES : (c + 1) * LANES] = e
                total = e if total is None else total + e
            tops.append(top)
            sums.append(total)
        tops = jnp.concatenate(tops, axis=0)
        sums = jnp.concatenate(sums, axis=0)
        f_ref[st, head] = tops
        row_top = jnp.max(tops, axis=1, keepdims=True)
        row_sum = jnp.sum(sums * jnp.exp2((tops - row_top) * scale_main), axis=1, keepdims=True)
        stm[...] = jnp.where(lane_rows == head, row_top, stm[...])
        stl[...] = jnp.where(lane_rows == head, row_sum, stl[...])

    def st_copy(st, i):
        return copy_to(st_tx.at[st], st_rx.at[st, i], st_s.at[st, i], st_r.at[st, i], ka_dev(i))

    def send_stats(st):
        st_tx[st, 0:heads] = jnp.transpose(stm[...], (1, 0))[0:heads]
        st_tx[st, heads : 2 * heads] = jnp.transpose(stl[...], (1, 0))[0:heads]
        for i in range(1, n_ka):
            st_copy(st, i).start()

    def finish(st):
        for i in range(1, n_ka):
            st_copy(st, i).wait_recv()
        tops = [st_tx[st, 0:heads]] + [st_rx[st, i, 0:heads] for i in range(1, n_ka)]
        sums = [st_tx[st, heads : 2 * heads]] + [st_rx[st, i, heads : 2 * heads] for i in range(1, n_ka)]
        top = functools.reduce(jnp.maximum, tops)
        total = functools.reduce(
            jnp.add, [b * jnp.exp2((a - top) * scale_main) for a, b in zip(tops, sums)]
        )
        comb[0:heads] = top
        comb[heads : 2 * heads] = 1.0 / (total * main_total)
        cols = jnp.transpose(comb[...], (1, 0))
        for head in range(heads):
            gtop = jnp.broadcast_to(cols[:, head : head + 1], (rows, LANES))
            ginv = jnp.broadcast_to(cols[:, heads + head : heads + head + 1], (rows, LANES))
            f_ref[st, head] = jnp.exp2((f_ref[st, head] - gtop) * scale_main) * ginv

        def one(g, carry):
            at = pl.ds(pl.multiple_of(g * 8, 8), 8)
            acc = [jnp.zeros((8, LANES), jnp.float32) for _ in range(tiles)]
            for head in range(heads):
                f = f_ref[st, head, at, :]
                slot = eslot(st, head)
                for c in range(tiles):
                    acc[c] = acc[c] + f * e_ref[slot, at, c * LANES : (c + 1) * LANES]
            spot = st * half + g // 4
            to = pl.ds(pl.multiple_of(lax.rem(g, 4) * 8, 8), 8)
            for c in range(tiles):
                part, inner = divmod(c, tiles // 2)
                t_ref[spot, part, to, inner * LANES : (inner + 1) * LANES] = acc[c]
            return carry

        lax.fori_loop(0, groups, one, 0)

    def spot_of(offset):
        return offsets.index(offset)

    def ra_copy(a, c):
        src = t_ref.at[spot_of(half if a == 0 else -(half - a)), c]
        return copy_to(src, rxa.at[a, c], ra_s.at[a, c], ra_r.at[a, c], ha_dev(-1))

    def rb_copy(a, c):
        src = t_ref.at[spot_of(half - a), c]
        return copy_to(src, rxb.at[a, c], rb_s.at[a, c], rb_r.at[a, c], ha_dev(1))

    def chain_a(a, c):
        if a > 1 or (a == 1 and c == 0):
            ra_copy(a - 1, c).wait_recv()
            spot = spot_of(-(half - a))
            t_ref[spot, c] = t_ref[spot, c] + rxa[a - 1, c]
        ra_copy(a, c).start()

    def chain_b(a, c):
        if a > 1 or (a == 1 and c == 1):
            rb_copy(a - 1, c).wait_recv()
            spot = spot_of(half - a)
            t_ref[spot, c] = t_ref[spot, c] + rxb[a - 1, c]
        rb_copy(a, c).start()

    def fwd(st, after, early):
        last = st == 1
        kcopy(0, 0).wait()
        scores(st, 0, 0, s0)
        kcopy(NBUF, 0).start()

        def pair(i, carry):
            h0 = 2 * i
            a = lax.rem(h0 + 1, NBUF)
            b = lax.rem(h0 + 2, NBUF)
            kcopy(h0 + 1, a).wait()
            kcopy(h0 + 2, b).wait()
            scores(st, h0 + 1, a, s1)
            soften(st, h0, s0)
            scores(st, h0 + 2, b, s0)
            soften(st, h0 + 1, s1)

            def refill():
                kcopy(lax.rem(h0 + 1 + NBUF, heads), a).start()
                kcopy(lax.rem(h0 + 2 + NBUF, heads), b).start()

            if last:
                pl.when(h0 + 1 + NBUF < heads)(lambda: kcopy(h0 + 1 + NBUF, a).start())
                pl.when(h0 + 2 + NBUF < heads)(lambda: kcopy(h0 + 2 + NBUF, b).start())
            else:
                refill()
            after(i)
            return carry

        if last:
            lax.fori_loop(0, heads // 2 - 1, pair, 0)
        else:
            lax.fori_loop(0, 1, pair, 0)
            early()
            lax.fori_loop(1, heads // 2 - 1, pair, 0)
        end = (heads - 1) % NBUF
        kcopy(heads - 1, end).wait()
        scores(st, heads - 1, end, s1)
        if not last:
            kcopy(NBUF - 1, end).start()
        soften(st, heads - 2, s0)
        soften(st, heads - 1, s1)

    fwd(0, lambda i: None, greet)
    send_stats(0)

    def beside(i):
        @pl.when(i == EXTRA // 2 - 1)
        def _():
            finish(0)
            chain_a(0, 0)
            chain_b(0, 1)
            chain_a(1, 1)
            chain_b(1, 0)

        @pl.when(i == EXTRA // 2 + 1)
        def _():
            chain_a(1, 0)
            chain_b(1, 1)

        @pl.when(i == EXTRA // 2 + 3)
        def _():
            chain_a(2, 1)
            chain_a(2, 0)

    fwd(1, beside, None)
    send_stats(1)

    iq_all[:, pl.ds(pl.multiple_of(h * 64, 64), 64), :] = iq_ref[:, pl.ds(pl.multiple_of(h * 64, 64), 64), :]
    wc_all[h] = wc_ref[h]
    ctx[pl.ds(pl.multiple_of(p * 256, 256), 256), :] = ik_ref[...]
    for i in range(1, n_pb):
        cx_copy(i).wait_recv()
    for i in range(1, n_ha):
        iq_copy(i).wait_recv()
        wc_copy(i).wait_recv()
    ctx_t[...] = jnp.transpose(ctx[...].astype(jnp.float32), (1, 0)).astype(jnp.bfloat16)
    for src in range(n_ha):
        for kk in range(n_ka // 2):
            spread = lane_spread(wc_all[src, kk : kk + 1, :])
            for one in range(2):
                w_rep[2 * kk + one, src * 64 : src * 64 + 64, :] = spread[one * 64 : one * 64 + 64]
        spread = lane_spread(wc_ref[src, pl.ds(k // 2, 1), :])
        w_own[src * 64 : src * 64 + 64, :] = jnp.where(lax.rem(k, 2) == 0, spread[0:64], spread[64:128])
    per = n_ha * 64
    for kk in range(n_ka):
        wq = jnp.transpose(w_rep[kk] * iq_all[kk].astype(jnp.float32), (1, 0))
        big = wq.astype(jnp.bfloat16)
        wq_t[0:128, kk * per : (kk + 1) * per] = big
        wq_t[128:256, kk * per : (kk + 1) * per] = (wq - big.astype(jnp.float32)).astype(jnp.bfloat16)

    finish(1)
    for c in range(2):
        chain_b(2, c)

    step = 512

    def index_part(n, carry):
        kk, sc = n // (keys // step), lax.rem(n, keys // step)
        at = pl.ds(pl.multiple_of(sc * step, step), step)
        act = jnp.dot(iq_all[kk], ctx_t[:, at], preferred_element_type=jnp.float32)
        w = w_rep[kk]
        parts = []
        for c in range(step // LANES):
            a = act[:, c * LANES : (c + 1) * LANES]
            r = jnp.maximum(a, 0.0) * w
            parts.append(jnp.sum(jnp.sum(r.reshape(n_ha, 64, LANES), axis=0).reshape(8, 8, LANES), axis=1))
        lg[kk, :, at] = jnp.concatenate(parts, axis=1) * scale
        m_ref[kk, :, at] = jnp.where(act > 0, 1.0, 0.0).astype(jnp.bfloat16)
        return carry

    total_parts = n_ka * (keys // step)
    lax.fori_loop(0, total_parts // 2, index_part, 0)
    for c in range(2):
        chain_a(3, c)
        chain_b(3, c)
    lax.fori_loop(total_parts // 2, total_parts, index_part, 0)

    rel = pos_ref[n_ha - 1][:, 0:1] - first_key
    seen = lax.broadcasted_iota(jnp.int32, (32, keys), 1) <= rel
    logits = jnp.where(seen, lg[...].reshape(32, keys), LOW)
    row_top = jnp.max(logits, axis=1, keepdims=True)
    expo = jnp.where(seen, jnp.exp(logits - row_top), 0.0)
    row_sum = jnp.sum(expo, axis=1, keepdims=True)
    lg[...] = expo.reshape(n_ka, 8, keys)
    ix_tx[0] = jnp.broadcast_to(row_top, (32, LANES))
    ix_tx[1] = jnp.broadcast_to(row_sum, (32, LANES))

    def ix_copy(i):
        return copy_to(ix_tx, ix_rx.at[i], ix_s.at[i], ix_r.at[i], ka_dev(i))

    for i in range(1, n_ka):
        ix_copy(i).start()
    for i in range(1, n_ka):
        ix_copy(i).wait_recv()
    tops = [ix_tx[0]] + [ix_rx[i, 0] for i in range(1, n_ka)]
    sums = [ix_tx[1]] + [ix_rx[i, 1] for i in range(1, n_ka)]
    top = functools.reduce(jnp.maximum, tops)
    total = functools.reduce(jnp.add, [b * jnp.exp(a - top) for a, b in zip(tops, sums)])
    factor = (jnp.exp(tops[0] - top) / total)[:, 0:1]

    for c in range(2):
        ra_copy(half - 1, c).wait_recv()
        rb_copy(half - 1, c).wait_recv()
        at = slice(c * (keys // 2), (c + 1) * (keys // 2))
        target = t_ref[n_ha - 1, c] + rxa[half - 1, c] + rxb[half - 1, c]
        diff = (lg[:, :, at].reshape(32, keys // 2) * factor - target) * (key_total / 16.0)
        big = diff.astype(jnp.bfloat16).astype(jnp.float32)
        small = diff - big
        for t in range(32):
            kk, r = divmod(t, 8)
            if r % 2:
                continue
            for value, ref in ((big, d_hi), (small, d_lo)):
                both = jnp.concatenate(
                    [
                        jnp.broadcast_to(value[t : t + 1], (8, keys // 2)),
                        jnp.broadcast_to(value[t + 1 : t + 2], (8, keys // 2)),
                    ],
                    axis=0,
                )
                ref[kk, r * 8 : r * 8 + 16, at] = both.astype(jnp.bfloat16)

    def gk_copy(i):
        return copy_to(gk_tx.at[i], gk_rx.at[i], gk_s.at[i], gk_r.at[i], pb_dev(i))

    def gated(kk, at, width, d_ref):
        return (m_ref[kk, :, at].reshape(n_ha, 64, width) * d_ref[kk, :, at][None]).reshape(per, width)

    def key_block(n, carry):
        i = n + 1
        dest = lax.rem(p + i, n_pb)
        at = pl.ds(pl.multiple_of(dest * 256, 256), 256)
        wide = jnp.zeros((256, 256), jnp.float32)
        thin = jnp.zeros((128, 256), jnp.float32)
        for kk in range(n_ka):
            hi = gated(kk, at, 256, d_hi)
            lo = gated(kk, at, 256, d_lo)
            wide += jnp.dot(wq_t[:, kk * per : (kk + 1) * per], hi, preferred_element_type=jnp.float32)
            thin += jnp.dot(wq_t[0:128, kk * per : (kk + 1) * per], lo, preferred_element_type=jnp.float32)
        block = (wide[0:128] + wide[128:256] + thin) * scale
        gk_tx[lax.rem(i, n_pb)] = jnp.transpose(block, (1, 0))

        @pl.when(i < n_pb)
        def _():
            gk_copy(i).start()

        return carry

    core, far = lax.rem(k, 2), k // 2

    def query_rows(kk):
        def block(n, total):
            at = pl.ds(pl.multiple_of(n * 512, 512), 512)
            key = ctx[at, :]
            return total + (
                jnp.dot(gated(kk, at, 512, d_hi), key, preferred_element_type=jnp.float32)
                + jnp.dot(gated(kk, at, 512, d_lo), key, preferred_element_type=jnp.float32)
            )

        u_ref[kk] = lax.fori_loop(0, keys // 512, block, jnp.zeros((per, 128), jnp.float32))

    def u_copy(x):
        return copy_to(
            u_ref.at[x * 2 + 1 - core], u_rx.at[x], u_s.at[x], u_r.at[x], {"ka": far * 2 + 1 - core}
        )

    v_copy = copy_to(v_ref.at[1 - far], v_rx, v_s.at[0], v_r.at[0], {"ka": (1 - far) * 2 + core})
    early_blocks = n_pb // 2
    lax.fori_loop(0, early_blocks, key_block, 0)
    for x in range(2):
        query_rows(x * 2 + 1 - core)
        u_copy(x).start()
    for first in range(2):
        x = 1 - far if first == 0 else far
        query_rows(x * 2 + core)
        u_copy(x).wait_recv()
        v_ref[x] = u_ref[x * 2 + core] + u_rx[x]
        if first == 0:
            v_copy.start()
    lax.fori_loop(early_blocks, n_pb, key_block, 0)

    v_copy.wait_recv()
    r_ref[...] = (v_ref[far] + v_rx[...]) * scale

    def o_copy(i):
        dest = lax.rem(h + i, n_ha)
        return copy_to(
            r_ref.at[pl.ds(pl.multiple_of(dest * 64, 64), 64), :], o_rx.at[h], o_s.at[i], o_r.at[i], ha_dev(i)
        )

    for i in range(1, n_ha):
        o_copy(i).start()

    own = gk_tx[0]
    for i in range(1, n_pb):
        gk_copy(i).wait_recv()
        own = own + gk_rx[i]
    z_tx[...] = own.reshape(n_ha, 256 // n_ha, 128)

    def z_copy(i):
        return copy_to(z_tx.at[lax.rem(h + i, n_ha)], z_rx.at[i], z_s.at[i], z_r.at[i], ha_dev(i))

    for i in range(1, n_ha):
        z_copy(i).start()

    mine = z_tx[h]
    for i in range(1, n_ha):
        z_copy(i).wait_recv()
        mine = mine + z_rx[i]
    zsum[h] = mine

    def y_copy(i):
        return copy_to(zsum.at[h], zsum.at[h], y_s.at[i], y_r.at[i], ha_dev(i))

    for i in range(1, n_ha):
        y_copy(i).start()

    o_rx[h] = r_ref[pl.ds(pl.multiple_of(h * 64, 64), 64), :]
    for i in range(1, n_ha):
        o_copy(i).wait_recv()
    for b in range(4):
        at = slice(b * LANES, (b + 1) * LANES)
        u = o_rx[2 * b : 2 * b + 2].reshape(LANES, 128)
        gq_ref[at, :] = u * w_own[at, :]
        dots = jnp.transpose(u * iq_ref[k, at, :].astype(jnp.float32), (1, 0))
        gw_ref[:, at] = jnp.broadcast_to(jnp.sum(dots, axis=0, keepdims=True), (8, LANES))

    for i in range(1, n_ha):
        y_copy(i).wait_recv()
    gk_ref[...] = zsum[...].reshape(256, 128)

    for i in range(1, n_pb):
        cx_copy(i).wait_send()
        gk_copy(i).wait_send()
    for i in range(1, n_ha):
        iq_copy(i).wait_send()
        wc_copy(i).wait_send()
        z_copy(i).wait_send()
        o_copy(i).wait_send()
        y_copy(i).wait_send()
    for i in range(1, n_ka):
        for st in range(2):
            st_copy(st, i).wait_send()
        ix_copy(i).wait_send()
    for a in range(half):
        for c in range(2):
            if a or c == 0:
                ra_copy(a, c).wait_send()
            if a or c == 1:
                rb_copy(a, c).wait_send()
    for x in range(2):
        u_copy(x).wait_send()
    v_copy.wait_send()


def body(sizes, main_query, main_key, index_query, index_weight, index_key, query_pos):
    n_pb, n_ha, n_ka = sizes
    t, heads, dh = main_query.shape
    keys = main_key.shape[0]
    joined = index_query.shape[1]
    dims = (n_pb, n_ha, n_ka, heads, dh, keys, heads * n_ha, keys * n_ka)
    qt = main_query.transpose(1, 2, 0)
    kt = main_key.transpose(1, 2, 0)
    iq = index_query.reshape(n_ka, n_ha * 64, 128)
    wc = index_weight.astype(jnp.float32).reshape(n_ka, n_ha, 64).transpose(1, 0, 2)
    wc = wc.reshape(n_ha, n_ka * 64 // LANES, LANES)
    pos = query_pos.astype(jnp.float32).reshape(n_ka, n_ha, 8).transpose(1, 0, 2).reshape(n_ha, 1, 32)
    pos = jnp.pad(pos, ((0, 0), (0, 7 - wc.shape[1]), (0, LANES - 32)))
    wc = jnp.concatenate([wc, pos], axis=1)

    half = n_ha // 2
    rows = half * 32
    per = n_ha * 64
    f32, bf16 = jnp.float32, jnp.bfloat16
    scratch = [
        pltpu.VMEM((heads, t, dh), bf16),
        pltpu.VMEM((t, dh), f32),
        pltpu.VMEM((n_ha, 32, LANES), jnp.int32),
        pltpu.VMEM((per, LANES), f32),
        pltpu.VMEM((NBUF, dh, keys), bf16),
        pltpu.VMEM((rows, keys), f32),
        pltpu.VMEM((rows, keys), f32),
        pltpu.VMEM((heads + EXTRA, rows, keys), f32),
        pltpu.VMEM((2, heads, rows, LANES), f32),
        pltpu.VMEM((rows, LANES), f32),
        pltpu.VMEM((rows, LANES), f32),
        pltpu.VMEM((2, 2 * heads, rows), f32),
        pltpu.VMEM((2, n_ka, 2 * heads, rows), f32),
        pltpu.VMEM((LANES, rows), f32),
        pltpu.VMEM((n_ha, 2, 32, keys // 2), f32),
        pltpu.VMEM((half, 2, 32, keys // 2), f32),
        pltpu.VMEM((half, 2, 32, keys // 2), f32),
        pltpu.VMEM((n_ka, per, 128), bf16),
        pltpu.VMEM((n_ha, 8, LANES), f32),
        pltpu.VMEM((n_ka, per, LANES), f32),
        pltpu.VMEM((256, n_ka * per), bf16),
        pltpu.VMEM((keys, 128), bf16),
        pltpu.VMEM((128, keys), bf16),
        pltpu.VMEM((n_ka, per, keys), bf16),
        pltpu.VMEM((n_ka, 8, keys), f32),
        pltpu.VMEM((n_ka, 64, keys), bf16),
        pltpu.VMEM((n_ka, 64, keys), bf16),
        pltpu.VMEM((2, 32, LANES), f32),
        pltpu.VMEM((n_ka, 2, 32, LANES), f32),
        pltpu.VMEM((n_ka, per, 128), f32),
        pltpu.VMEM((2, per, 128), f32),
        pltpu.VMEM((2, per, 128), f32),
        pltpu.VMEM((per, 128), f32),
        pltpu.VMEM((per, 128), f32),
        pltpu.VMEM((n_ha, 64, 128), f32),
        pltpu.VMEM((n_pb, 256, 128), f32),
        pltpu.VMEM((n_pb, 256, 128), f32),
        pltpu.VMEM((n_ha, 256 // n_ha, 128), f32),
        pltpu.VMEM((n_ha, 256 // n_ha, 128), f32),
        pltpu.VMEM((n_ha, 256 // n_ha, 128), f32),
    ]
    dma = pltpu.SemaphoreType.DMA
    sems = [dma((NBUF,))]
    for shape in (
        (2, n_ka), (half, 2), (half, 2), (n_ha,), (n_ha,), (n_pb,),
        (n_ka,), (2,), (1,), (n_ha,), (n_pb,), (n_ha,), (n_ha,),
    ):
        sems += [dma(shape), dma(shape)]
    vmem = pl.BlockSpec(memory_space=pltpu.VMEM)
    gq, gw, gk = pl.pallas_call(
        functools.partial(kernel, dims),
        out_shape=(
            jax.ShapeDtypeStruct((per, 128), f32),
            jax.ShapeDtypeStruct((8, per), f32),
            jax.ShapeDtypeStruct((256, 128), f32),
        ),
        in_specs=[vmem, pl.BlockSpec(memory_space=pl.ANY)] + [vmem] * 3,
        out_specs=(vmem, vmem, vmem),
        scratch_shapes=scratch + sems,
        compiler_params=pltpu.CompilerParams(
            collective_id=0, has_side_effects=True, vmem_limit_bytes=63 * 1024 * 1024
        ),
    )(qt, kt, iq, wc, index_key)
    return (gq.reshape(t // n_ka, joined, 128), gw[0].reshape(t // n_ka, joined), gk)


def solution(mesh):
    placed = (
        P("pb", "ha", None),
        P("ka", "ha", None),
        P("pb", "ha", None),
        P("pb", "ha"),
        P(("pb", "ka"), None),
        P("pb"),
    )
    sizes = tuple(mesh.shape[name] for name in ("pb", "ha", "ka"))
    return jax.shard_map(
        functools.partial(body, sizes),
        mesh=mesh,
        in_specs=placed,
        out_specs=(P(("pb", "ka"), "ha", None), P(("pb", "ka"), "ha"), P(("pb", "ka"), None)),
        check_vma=False,
    )
```

```python
import functools
import math

import jax
import jax.numpy as jnp
from jax import lax
from jax.experimental import pallas as pl
from jax.experimental.pallas import tpu as pltpu
from jax.sharding import PartitionSpec as P

MESH = pl.DeviceIdType.MESH
LOW = -1e30
LANES = 128
NBUF = 4
EXTRA = 6
LOG2E = 1.4426950408889634


def stages(n_ha):
    half = n_ha // 2
    firsts = (0, half - 1, half + 1, n_ha)
    return firsts, 32 * max(b - a for a, b in zip(firsts, firsts[1:]))


def lane_spread(row):
    return jnp.transpose(jnp.broadcast_to(row, (LANES, LANES)), (1, 0))


def kernel(
    dims,
    qt_ref, kt_ref, iq_ref, wc_ref, ik_ref,
    gq_ref, gw_ref, gk_ref,
    q_ref, q_wide, pos_ref, w_own, kbuf, s0, s1, e_ref, f_ref, stm, stl, st_tx, st_rx, comb,
    t_ref, rxa, rxb,
    iq_all, wc_all, w_rep, wq_t, ctx, ctx_t, m_ref, lg, d_hi, d_lo,
    ix_tx, ix_rx,
    u_ref, u_rx, v_ref, v_rx, r_ref, o_rx,
    gk_tx, gk_rx, z_tx, z_rx, zsum,
    ksem, st_s, st_r, ra_s, ra_r, rb_s, rb_r, iq_s, iq_r, wc_s, wc_r, cx_s, cx_r,
    ix_s, ix_r, u_s, u_r, v_s, v_r, o_s, o_r, gk_s, gk_r, z_s, z_r, y_s, y_r,
):
    n_pb, n_ha, n_ka, heads, dh, keys, main_total, key_total = dims
    p, h, k = lax.axis_index("pb"), lax.axis_index("ha"), lax.axis_index("ka")
    half = n_ha // 2
    firsts, most = stages(n_ha)
    spans = [(firsts[st], firsts[st + 1]) for st in range(len(firsts) - 1)]
    tiles = keys // LANES
    slots = heads + EXTRA
    scale_main = LOG2E / math.sqrt(dh)
    scale = 1.0 / math.sqrt(128)

    offsets = [half]
    for o in range(half - 1, 0, -1):
        offsets += [-o, o]
    offsets += [0]

    def copy_to(src, dst, ss, rs, dev):
        return pltpu.make_async_remote_copy(
            src_ref=src, dst_ref=dst, send_sem=ss, recv_sem=rs, device_id=dev, device_id_type=MESH
        )

    def pb_dev(i):
        return {"pb": lax.rem(p + i, n_pb)}

    def ha_dev(i):
        return {"ha": lax.rem(h + i + n_ha, n_ha)}

    def ka_dev(i):
        return {"ka": lax.rem(k + i, n_ka)}

    def kcopy(head, slot):
        return pltpu.make_async_copy(kt_ref.at[head], kbuf.at[slot], ksem.at[slot])

    for n in range(NBUF):
        kcopy(n, n).start()

    barrier = pltpu.get_barrier_semaphore()
    for i in range(1, n_ha):
        pl.semaphore_signal(barrier, inc=1, device_id=ha_dev(i), device_id_type=MESH)
    for i in range(1, n_pb):
        pl.semaphore_signal(barrier, inc=1, device_id=pb_dev(i), device_id_type=MESH)
    for i in range(1, n_ka):
        pl.semaphore_signal(barrier, inc=1, device_id=ka_dev(i), device_id_type=MESH)
    def iq_copy(i):
        dest = lax.rem(h + i, n_ha)
        return copy_to(
            iq_ref.at[:, pl.ds(pl.multiple_of(dest * 64, 64), 64), :],
            iq_all.at[:, pl.ds(pl.multiple_of(h * 64, 64), 64), :],
            iq_s.at[i], iq_r.at[i], ha_dev(i),
        )

    def wc_copy(i):
        dest = lax.rem(h + i, n_ha)
        return copy_to(wc_ref.at[dest], wc_all.at[h], wc_s.at[i], wc_r.at[i], ha_dev(i))

    def cx_copy(i):
        return copy_to(
            ik_ref, ctx.at[pl.ds(pl.multiple_of(p * 256, 256), 256), :], cx_s.at[i], cx_r.at[i], pb_dev(i)
        )

    def greet():
        pl.semaphore_wait(barrier, n_ha + n_pb + n_ka - 3)
        for i in range(1, n_pb):
            cx_copy(i).start()
        for i in range(1, n_ha):
            iq_copy(i).start()
            wc_copy(i).start()

    lane = lax.broadcasted_iota(jnp.int32, (8, LANES), 1)
    for ref in (stm, stl):
        ref[...] = jnp.zeros_like(ref)
    first_key = k * keys

    def dest_of(i):
        return lax.rem(h + offsets[i] + n_ha, n_ha)

    for i in range(n_ha):
        pos_ref[i] = lane_spread(wc_ref[dest_of(i), 2:3, :])[0:32].astype(jnp.int32)

    def order_queries(head, carry):
        q_wide[...] = jnp.transpose(qt_ref[head].astype(jnp.float32), (1, 0))
        for i in range(n_ha):
            chunk = [
                q_wide[pl.ds(pl.multiple_of(kk * n_ha * 8 + dest_of(i) * 8, 8), 8), :] for kk in range(n_ka)
            ]
            q_ref[head, i * 32 : i * 32 + 32, :] = jnp.concatenate(chunk, axis=0).astype(jnp.bfloat16)
        return carry

    lax.fori_loop(0, heads, order_queries, 0)

    def scores(st, head, slot, out):
        lo, hi = spans[st]
        q = q_ref[head, lo * 32 : hi * 32, :]
        out[0 : (hi - lo) * 32] = jnp.dot(q, kbuf[slot], preferred_element_type=jnp.float32)

    def eslot(st, head):
        return lax.rem(st * heads + head, slots) if not isinstance(head, int) else (st * heads + head) % slots

    def soften(st, head, src):
        slot = eslot(st, head)
        lo, hi = spans[st]
        rows = (hi - lo) * 32
        span = slice(lo * 32, hi * 32)
        tops, sums = [], []
        for g in range(rows // 8):
            rel = pos_ref[lo + g // 4, (g % 4) * 8 : (g % 4) * 8 + 8, :] - first_key - lane
            x = [
                jnp.where(rel >= c * LANES, src[g * 8 : g * 8 + 8, c * LANES : (c + 1) * LANES], LOW)
                for c in range(tiles)
            ]
            top = functools.reduce(jnp.maximum, x)
            total = None
            for c in range(tiles):
                e = jnp.exp2((x[c] - top) * scale_main)
                e_ref[slot, g * 8 : g * 8 + 8, c * LANES : (c + 1) * LANES] = e
                total = e if total is None else total + e
            tops.append(top)
            sums.append(total)
        tops = jnp.concatenate(tops, axis=0)
        sums = jnp.concatenate(sums, axis=0)
        f_ref[head, span] = tops
        row_top = jnp.max(tops, axis=1, keepdims=True)
        row_sum = jnp.sum(sums * jnp.exp2((tops - row_top) * scale_main), axis=1, keepdims=True)
        here = lax.broadcasted_iota(jnp.int32, (rows, LANES), 1) == head
        stm[span] = jnp.where(here, row_top, stm[span])
        stl[span] = jnp.where(here, row_sum, stl[span])

    def st_copy(st, i):
        return copy_to(st_tx.at[st], st_rx.at[st, i], st_s.at[st, i], st_r.at[st, i], ka_dev(i))

    def send_stats(st):
        st_tx[st, 0:heads] = jnp.transpose(stm[...], (1, 0))[0:heads]
        st_tx[st, heads : 2 * heads] = jnp.transpose(stl[...], (1, 0))[0:heads]
        for i in range(1, n_ka):
            st_copy(st, i).start()

    def finish(st):
        for i in range(1, n_ka):
            st_copy(st, i).wait_recv()
        tops = [st_tx[st, 0:heads]] + [st_rx[st, i, 0:heads] for i in range(1, n_ka)]
        sums = [st_tx[st, heads : 2 * heads]] + [st_rx[st, i, heads : 2 * heads] for i in range(1, n_ka)]
        top = functools.reduce(jnp.maximum, tops)
        total = functools.reduce(
            jnp.add, [b * jnp.exp2((a - top) * scale_main) for a, b in zip(tops, sums)]
        )
        comb[0:heads] = top
        comb[heads : 2 * heads] = 1.0 / (total * main_total)
        lo, hi = spans[st]
        rows = (hi - lo) * 32
        span = slice(lo * 32, hi * 32)
        cols = jnp.transpose(comb[...], (1, 0))[span]
        for head in range(heads):
            gtop = jnp.broadcast_to(cols[:, head : head + 1], (rows, LANES))
            ginv = jnp.broadcast_to(cols[:, heads + head : heads + head + 1], (rows, LANES))
            f_ref[head, span] = jnp.exp2((f_ref[head, span] - gtop) * scale_main) * ginv

        def one(g, carry):
            at = pl.ds(pl.multiple_of(g * 8, 8), 8)
            acc = [jnp.zeros((8, LANES), jnp.float32) for _ in range(tiles)]
            for head in range(heads):
                f = f_ref[head, pl.ds(pl.multiple_of(lo * 32 + g * 8, 8), 8), :]
                slot = eslot(st, head)
                for c in range(tiles):
                    acc[c] = acc[c] + f * e_ref[slot, at, c * LANES : (c + 1) * LANES]
            spot = lo + g // 4
            to = pl.ds(pl.multiple_of(lax.rem(g, 4) * 8, 8), 8)
            for c in range(tiles):
                part, inner = divmod(c, tiles // 2)
                t_ref[spot, part, to, inner * LANES : (inner + 1) * LANES] = acc[c]
            return carry

        lax.fori_loop(0, rows // 8, one, 0)

    def spot_of(offset):
        return offsets.index(offset)

    def ra_copy(a, c):
        src = t_ref.at[spot_of(half if a == 0 else -(half - a)), c]
        return copy_to(src, rxa.at[a, c], ra_s.at[a, c], ra_r.at[a, c], ha_dev(-1))

    def rb_copy(a, c):
        src = t_ref.at[spot_of(half - a), c]
        return copy_to(src, rxb.at[a, c], rb_s.at[a, c], rb_r.at[a, c], ha_dev(1))

    def chain_a(a, c):
        if a > 1 or (a == 1 and c == 0):
            ra_copy(a - 1, c).wait_recv()
            spot = spot_of(-(half - a))
            t_ref[spot, c] = t_ref[spot, c] + rxa[a - 1, c]
        ra_copy(a, c).start()

    def chain_b(a, c):
        if a > 1 or (a == 1 and c == 1):
            rb_copy(a - 1, c).wait_recv()
            spot = spot_of(half - a)
            t_ref[spot, c] = t_ref[spot, c] + rxb[a - 1, c]
        rb_copy(a, c).start()

    def fwd(st, after, early):
        last = st == len(spans) - 1
        kcopy(0, 0).wait()
        scores(st, 0, 0, s0)
        kcopy(NBUF, 0).start()

        def pair(i, carry):
            h0 = 2 * i
            a = lax.rem(h0 + 1, NBUF)
            b = lax.rem(h0 + 2, NBUF)
            kcopy(h0 + 1, a).wait()
            kcopy(h0 + 2, b).wait()
            scores(st, h0 + 1, a, s1)
            soften(st, h0, s0)
            scores(st, h0 + 2, b, s0)
            soften(st, h0 + 1, s1)

            def refill():
                kcopy(lax.rem(h0 + 1 + NBUF, heads), a).start()
                kcopy(lax.rem(h0 + 2 + NBUF, heads), b).start()

            if last:
                pl.when(h0 + 1 + NBUF < heads)(lambda: kcopy(h0 + 1 + NBUF, a).start())
                pl.when(h0 + 2 + NBUF < heads)(lambda: kcopy(h0 + 2 + NBUF, b).start())
            else:
                refill()
            after(i)
            return carry

        if early is None:
            lax.fori_loop(0, heads // 2 - 1, pair, 0)
        else:
            lax.fori_loop(0, 1, pair, 0)
            early()
            lax.fori_loop(1, heads // 2 - 1, pair, 0)
        end = (heads - 1) % NBUF
        kcopy(heads - 1, end).wait()
        scores(st, heads - 1, end, s1)
        if not last:
            kcopy(NBUF - 1, end).start()
        soften(st, heads - 2, s0)
        soften(st, heads - 1, s1)

    fwd(0, lambda i: None, greet)
    send_stats(0)

    def beside(i):
        @pl.when(i == EXTRA // 2 - 1)
        def _():
            finish(0)
            chain_a(0, 0)
            chain_b(0, 1)
            chain_a(1, 1)
            chain_b(1, 0)

    def beside_last(i):
        @pl.when(i == 1)
        def _():
            chain_a(1, 0)
            chain_b(1, 1)

        @pl.when(i == EXTRA // 2 - 1)
        def _():
            finish(1)

    fwd(1, beside, None)
    send_stats(1)
    fwd(2, beside_last, None)
    send_stats(2)

    iq_all[:, pl.ds(pl.multiple_of(h * 64, 64), 64), :] = iq_ref[:, pl.ds(pl.multiple_of(h * 64, 64), 64), :]
    wc_all[h] = wc_ref[h]
    ctx[pl.ds(pl.multiple_of(p * 256, 256), 256), :] = ik_ref[...]
    for i in range(1, n_pb):
        cx_copy(i).wait_recv()
    for i in range(1, n_ha):
        iq_copy(i).wait_recv()
        wc_copy(i).wait_recv()
    ctx_t[...] = jnp.transpose(ctx[...].astype(jnp.float32), (1, 0)).astype(jnp.bfloat16)
    for src in range(n_ha):
        for kk in range(n_ka // 2):
            spread = lane_spread(wc_all[src, kk : kk + 1, :])
            for one in range(2):
                w_rep[2 * kk + one, src * 64 : src * 64 + 64, :] = spread[one * 64 : one * 64 + 64]
        spread = lane_spread(wc_ref[src, pl.ds(k // 2, 1), :])
        w_own[src * 64 : src * 64 + 64, :] = jnp.where(lax.rem(k, 2) == 0, spread[0:64], spread[64:128])
    per = n_ha * 64
    for kk in range(n_ka):
        wq = jnp.transpose(w_rep[kk] * iq_all[kk].astype(jnp.float32), (1, 0))
        big = wq.astype(jnp.bfloat16)
        wq_t[0:128, kk * per : (kk + 1) * per] = big
        wq_t[128:256, kk * per : (kk + 1) * per] = (wq - big.astype(jnp.float32)).astype(jnp.bfloat16)

    step = 512

    def index_part(n, carry):
        kk, sc = n // (keys // step), lax.rem(n, keys // step)
        at = pl.ds(pl.multiple_of(sc * step, step), step)
        act = jnp.dot(iq_all[kk], ctx_t[:, at], preferred_element_type=jnp.float32)
        w = w_rep[kk]
        parts = []
        for c in range(step // LANES):
            a = act[:, c * LANES : (c + 1) * LANES]
            r = jnp.maximum(a, 0.0) * w
            parts.append(jnp.sum(jnp.sum(r.reshape(n_ha, 64, LANES), axis=0).reshape(8, 8, LANES), axis=1))
        lg[kk, :, at] = jnp.concatenate(parts, axis=1) * scale
        m_ref[kk, :, at] = jnp.where(act > 0, 1.0, 0.0).astype(jnp.bfloat16)
        return carry

    total_parts = n_ka * (keys // step)
    for c in (1, 0):
        chain_a(2, c)
        chain_b(2, 1 - c)
    lax.fori_loop(0, total_parts // 4, index_part, 0)
    finish(2)
    lax.fori_loop(total_parts // 4, total_parts, index_part, 0)
    for c in range(2):
        chain_a(3, c)
        chain_b(3, c)

    rel = pos_ref[n_ha - 1][:, 0:1] - first_key
    seen = lax.broadcasted_iota(jnp.int32, (32, keys), 1) <= rel
    logits = jnp.where(seen, lg[...].reshape(32, keys), LOW)
    row_top = jnp.max(logits, axis=1, keepdims=True)
    expo = jnp.where(seen, jnp.exp(logits - row_top), 0.0)
    row_sum = jnp.sum(expo, axis=1, keepdims=True)
    lg[...] = expo.reshape(n_ka, 8, keys)
    ix_tx[0] = jnp.broadcast_to(row_top, (32, LANES))
    ix_tx[1] = jnp.broadcast_to(row_sum, (32, LANES))

    def ix_copy(i):
        return copy_to(ix_tx, ix_rx.at[i], ix_s.at[i], ix_r.at[i], ka_dev(i))

    for i in range(1, n_ka):
        ix_copy(i).start()
    for i in range(1, n_ka):
        ix_copy(i).wait_recv()
    tops = [ix_tx[0]] + [ix_rx[i, 0] for i in range(1, n_ka)]
    sums = [ix_tx[1]] + [ix_rx[i, 1] for i in range(1, n_ka)]
    top = functools.reduce(jnp.maximum, tops)
    total = functools.reduce(jnp.add, [b * jnp.exp(a - top) for a, b in zip(tops, sums)])
    factor = (jnp.exp(tops[0] - top) / total)[:, 0:1]

    def diff_half(c):
        ra_copy(half - 1, c).wait_recv()
        rb_copy(half - 1, c).wait_recv()
        at = slice(c * (keys // 2), (c + 1) * (keys // 2))
        target = t_ref[n_ha - 1, c] + rxa[half - 1, c] + rxb[half - 1, c]
        diff = (lg[:, :, at].reshape(32, keys // 2) * factor - target) * (key_total / 16.0)
        big = diff.astype(jnp.bfloat16).astype(jnp.float32)
        small = diff - big
        for t in range(32):
            kk, r = divmod(t, 8)
            if r % 2:
                continue
            for value, ref in ((big, d_hi), (small, d_lo)):
                both = jnp.concatenate(
                    [
                        jnp.broadcast_to(value[t : t + 1], (8, keys // 2)),
                        jnp.broadcast_to(value[t + 1 : t + 2], (8, keys // 2)),
                    ],
                    axis=0,
                )
                ref[kk, r * 8 : r * 8 + 16, at] = both.astype(jnp.bfloat16)

    def gk_copy(i):
        return copy_to(gk_tx.at[i], gk_rx.at[i], gk_s.at[i], gk_r.at[i], pb_dev(i))

    def gated(kk, at, width, d_ref):
        return (m_ref[kk, :, at].reshape(n_ha, 64, width) * d_ref[kk, :, at][None]).reshape(per, width)

    def key_block(n, carry):
        dest = (n // many) * many + lax.rem(p + n, many)
        i = lax.rem(dest - p + n_pb, n_pb)
        at = pl.ds(pl.multiple_of(dest * 256, 256), 256)
        wide = jnp.zeros((256, 256), jnp.float32)
        thin = jnp.zeros((128, 256), jnp.float32)
        for kk in range(n_ka):
            hi = gated(kk, at, 256, d_hi)
            lo = gated(kk, at, 256, d_lo)
            wide += jnp.dot(wq_t[:, kk * per : (kk + 1) * per], hi, preferred_element_type=jnp.float32)
            thin += jnp.dot(wq_t[0:128, kk * per : (kk + 1) * per], lo, preferred_element_type=jnp.float32)
        block = (wide[0:128] + wide[128:256] + thin) * scale
        gk_tx[i] = jnp.transpose(block, (1, 0))

        @pl.when(i > 0)
        def _():
            gk_copy(i).start()

        return carry

    many = n_pb // 2
    for c in range(2):
        diff_half(c)
        lax.fori_loop(c * many, (c + 1) * many, key_block, 0)

    core, far = lax.rem(k, 2), k // 2

    def query_rows(part, kk):
        mask = jnp.concatenate(
            [m_ref[kk, src * 64 + part * 32 : src * 64 + part * 32 + 32, :] for src in range(n_ha)], axis=0
        ).reshape(n_ha, 32, keys)
        hi = (mask * d_hi[kk, part * 32 : part * 32 + 32, :][None]).reshape(n_ha * 32, keys)
        lo = (mask * d_lo[kk, part * 32 : part * 32 + 32, :][None]).reshape(n_ha * 32, keys)
        key = ctx[...]
        u_ref[part, kk] = jnp.dot(hi, key, preferred_element_type=jnp.float32) + jnp.dot(
            lo, key, preferred_element_type=jnp.float32
        )

    def u_copy(part, x):
        return copy_to(
            u_ref.at[part, x * 2 + 1 - core], u_rx.at[part, x], u_s.at[part, x], u_r.at[part, x],
            {"ka": far * 2 + 1 - core},
        )

    def v_copy(part):
        return copy_to(
            v_ref.at[part, 1 - far], v_rx.at[part], v_s.at[part], v_r.at[part], {"ka": (1 - far) * 2 + core}
        )

    def o_copy(part, i):
        dest = lax.rem(h + i, n_ha)
        return copy_to(
            r_ref.at[part, pl.ds(pl.multiple_of(dest * 32, 32), 32), :],
            o_rx.at[h, part * 32 : part * 32 + 32, :],
            o_s.at[part, i], o_r.at[part, i], ha_dev(i),
        )

    def z_copy(i):
        return copy_to(z_tx.at[lax.rem(h + i, n_ha)], z_rx.at[i], z_s.at[i], z_r.at[i], ha_dev(i))

    def y_copy(i):
        return copy_to(zsum.at[h], zsum.at[h], y_s.at[i], y_r.at[i], ha_dev(i))

    def other_core(part):
        for x in range(2):
            query_rows(part, x * 2 + 1 - core)
            u_copy(part, x).start()

    def own_core(part):
        for first in range(2):
            x = 1 - far if first == 0 else far
            query_rows(part, x * 2 + core)
            u_copy(part, x).wait_recv()
            v_ref[part, x] = u_ref[part, x * 2 + core] + u_rx[part, x]
            if first == 0:
                v_copy(part).start()

    def to_owners(part):
        v_copy(part).wait_recv()
        r_ref[part] = (v_ref[part, far] + v_rx[part]) * scale
        for i in range(1, n_ha):
            o_copy(part, i).start()
        o_rx[h, part * 32 : part * 32 + 32, :] = r_ref[part, pl.ds(pl.multiple_of(h * 32, 32), 32), :]

    other_core(0)
    own_core(0)
    other_core(1)
    to_owners(0)

    own = gk_tx[0]
    for i in range(1, n_pb):
        gk_copy(i).wait_recv()
        own = own + gk_rx[i]
    z_tx[...] = own.reshape(n_ha, 256 // n_ha, 128)
    for i in range(1, n_ha):
        z_copy(i).start()

    own_core(1)
    mine = z_tx[h]
    for i in range(1, n_ha):
        z_copy(i).wait_recv()
        mine = mine + z_rx[i]
    zsum[h] = mine
    for i in range(1, n_ha):
        y_copy(i).start()
    to_owners(1)

    for part in range(2):
        for i in range(1, n_ha):
            o_copy(part, i).wait_recv()
    for b in range(4):
        at = slice(b * LANES, (b + 1) * LANES)
        u = o_rx[2 * b : 2 * b + 2].reshape(LANES, 128)
        gq_ref[at, :] = u * w_own[at, :]
        dots = jnp.transpose(u * iq_ref[k, at, :].astype(jnp.float32), (1, 0))
        gw_ref[:, at] = jnp.broadcast_to(jnp.sum(dots, axis=0, keepdims=True), (8, LANES))

    for i in range(1, n_ha):
        y_copy(i).wait_recv()
    gk_ref[...] = zsum[...].reshape(256, 128)

    for i in range(1, n_pb):
        cx_copy(i).wait_send()
        gk_copy(i).wait_send()
    for i in range(1, n_ha):
        iq_copy(i).wait_send()
        wc_copy(i).wait_send()
        z_copy(i).wait_send()
        for part in range(2):
            o_copy(part, i).wait_send()
        y_copy(i).wait_send()
    for i in range(1, n_ka):
        for st in range(len(spans)):
            st_copy(st, i).wait_send()
        ix_copy(i).wait_send()
    for a in range(half):
        for c in range(2):
            if a or c == 0:
                ra_copy(a, c).wait_send()
            if a or c == 1:
                rb_copy(a, c).wait_send()
    for part in range(2):
        for x in range(2):
            u_copy(part, x).wait_send()
        v_copy(part).wait_send()


def body(sizes, main_query, main_key, index_query, index_weight, index_key, query_pos):
    n_pb, n_ha, n_ka = sizes
    t, heads, dh = main_query.shape
    keys = main_key.shape[0]
    joined = index_query.shape[1]
    dims = (n_pb, n_ha, n_ka, heads, dh, keys, heads * n_ha, keys * n_ka)
    qt = main_query.transpose(1, 2, 0)
    kt = main_key.transpose(1, 2, 0)
    iq = index_query.reshape(n_ka, n_ha * 64, 128)
    wc = index_weight.astype(jnp.float32).reshape(n_ka, n_ha, 64).transpose(1, 0, 2)
    wc = wc.reshape(n_ha, n_ka * 64 // LANES, LANES)
    pos = query_pos.astype(jnp.float32).reshape(n_ka, n_ha, 8).transpose(1, 0, 2).reshape(n_ha, 1, 32)
    pos = jnp.pad(pos, ((0, 0), (0, 7 - wc.shape[1]), (0, LANES - 32)))
    wc = jnp.concatenate([wc, pos], axis=1)

    half = n_ha // 2
    firsts, rows = stages(n_ha)
    n_st = len(firsts) - 1
    per = n_ha * 64
    f32, bf16 = jnp.float32, jnp.bfloat16
    scratch = [
        pltpu.VMEM((heads, t, dh), bf16),
        pltpu.VMEM((t, dh), f32),
        pltpu.VMEM((n_ha, 32, LANES), jnp.int32),
        pltpu.VMEM((per, LANES), f32),
        pltpu.VMEM((NBUF, dh, keys), bf16),
        pltpu.VMEM((rows, keys), f32),
        pltpu.VMEM((rows, keys), f32),
        pltpu.VMEM((heads + EXTRA, rows, keys), f32),
        pltpu.VMEM((heads, t, LANES), f32),
        pltpu.VMEM((t, LANES), f32),
        pltpu.VMEM((t, LANES), f32),
        pltpu.VMEM((n_st, 2 * heads, t), f32),
        pltpu.VMEM((n_st, n_ka, 2 * heads, t), f32),
        pltpu.VMEM((LANES, t), f32),
        pltpu.VMEM((n_ha, 2, 32, keys // 2), f32),
        pltpu.VMEM((half, 2, 32, keys // 2), f32),
        pltpu.VMEM((half, 2, 32, keys // 2), f32),
        pltpu.VMEM((n_ka, per, 128), bf16),
        pltpu.VMEM((n_ha, 8, LANES), f32),
        pltpu.VMEM((n_ka, per, LANES), f32),
        pltpu.VMEM((256, n_ka * per), bf16),
        pltpu.VMEM((keys, 128), bf16),
        pltpu.VMEM((128, keys), bf16),
        pltpu.VMEM((n_ka, per, keys), bf16),
        pltpu.VMEM((n_ka, 8, keys), f32),
        pltpu.VMEM((n_ka, 64, keys), bf16),
        pltpu.VMEM((n_ka, 64, keys), bf16),
        pltpu.VMEM((2, 32, LANES), f32),
        pltpu.VMEM((n_ka, 2, 32, LANES), f32),
        pltpu.VMEM((2, n_ka, per // 2, 128), f32),
        pltpu.VMEM((2, 2, per // 2, 128), f32),
        pltpu.VMEM((2, 2, per // 2, 128), f32),
        pltpu.VMEM((2, per // 2, 128), f32),
        pltpu.VMEM((2, per // 2, 128), f32),
        pltpu.VMEM((n_ha, 64, 128), f32),
        pltpu.VMEM((n_pb, 256, 128), f32),
        pltpu.VMEM((n_pb, 256, 128), f32),
        pltpu.VMEM((n_ha, 256 // n_ha, 128), f32),
        pltpu.VMEM((n_ha, 256 // n_ha, 128), f32),
        pltpu.VMEM((n_ha, 256 // n_ha, 128), f32),
    ]
    dma = pltpu.SemaphoreType.DMA
    sems = [dma((NBUF,))]
    for shape in (
        (n_st, n_ka), (half, 2), (half, 2), (n_ha,), (n_ha,), (n_pb,),
        (n_ka,), (2, 2), (2,), (2, n_ha), (n_pb,), (n_ha,), (n_ha,),
    ):
        sems += [dma(shape), dma(shape)]
    vmem = pl.BlockSpec(memory_space=pltpu.VMEM)
    gq, gw, gk = pl.pallas_call(
        functools.partial(kernel, dims),
        out_shape=(
            jax.ShapeDtypeStruct((per, 128), f32),
            jax.ShapeDtypeStruct((8, per), f32),
            jax.ShapeDtypeStruct((256, 128), f32),
        ),
        in_specs=[vmem, pl.BlockSpec(memory_space=pl.ANY)] + [vmem] * 3,
        out_specs=(vmem, vmem, vmem),
        scratch_shapes=scratch + sems,
        compiler_params=pltpu.CompilerParams(
            collective_id=0, has_side_effects=True, vmem_limit_bytes=63 * 1024 * 1024
        ),
    )(qt, kt, iq, wc, index_key)
    return (gq.reshape(t // n_ka, joined, 128), gw[0].reshape(t // n_ka, joined), gk)


def solution(mesh):
    placed = (
        P("pb", "ha", None),
        P("ka", "ha", None),
        P("pb", "ha", None),
        P("pb", "ha"),
        P(("pb", "ka"), None),
        P("pb"),
    )
    sizes = tuple(mesh.shape[name] for name in ("pb", "ha", "ka"))
    return jax.shard_map(
        functools.partial(body, sizes),
        mesh=mesh,
        in_specs=placed,
        out_specs=(P(("pb", "ka"), "ha", None), P(("pb", "ka"), "ha"), P(("pb", "ka"), None)),
        check_vma=False,
    )
```

```python
import functools
import math

import jax
import jax.numpy as jnp
from jax import lax
from jax.experimental import pallas as pl
from jax.experimental.pallas import tpu as pltpu
from jax.sharding import PartitionSpec as P

MESH = pl.DeviceIdType.MESH
LOW = -1e30
LANES = 128
NBUF = 4
EXTRA = 6
LOG2E = 1.4426950408889634


def stages(n_ha):
    half = n_ha // 2
    firsts = (0, half - 1, half + 1, n_ha)
    return firsts, 32 * max(b - a for a, b in zip(firsts, firsts[1:]))


def lane_spread(row):
    return jnp.transpose(jnp.broadcast_to(row, (LANES, LANES)), (1, 0))


def kernel(
    dims,
    qt_ref, kt_ref, iq_ref, wc_ref, ik_ref,
    gq_ref, gw_ref, gk_ref,
    q_ref, q_wide, pos_ref, w_own, kbuf, s0, s1, e_ref, f_ref, stm, stl, st_tx, st_rx, comb,
    t_ref, rxa, rxb,
    iq_all, wc_all, w_rep, wq_t, ctx, ctx_t, m_ref, lg, d_hi, d_lo,
    ix_tx, ix_rx,
    u_ref, u_rx, v_ref, v_rx, r_ref, o_rx,
    gk_tx, gk_rx, z_tx, z_rx, zsum,
    ksem, st_s, st_r, ra_s, ra_r, rb_s, rb_r, iq_s, iq_r, wc_s, wc_r, cx_s, cx_r,
    ix_s, ix_r, u_s, u_r, v_s, v_r, o_s, o_r, gk_s, gk_r, z_s, z_r, y_s, y_r,
):
    n_pb, n_ha, n_ka, heads, dh, keys, main_total, key_total = dims
    p, h, k = lax.axis_index("pb"), lax.axis_index("ha"), lax.axis_index("ka")
    half = n_ha // 2
    firsts, most = stages(n_ha)
    spans = [(firsts[st], firsts[st + 1]) for st in range(len(firsts) - 1)]
    tiles = keys // LANES
    slots = heads + EXTRA
    scale_main = LOG2E / math.sqrt(dh)
    scale = 1.0 / math.sqrt(128)

    offsets = [half]
    for o in range(half - 1, 0, -1):
        offsets += [-o, o]
    offsets += [0]

    def copy_to(src, dst, ss, rs, dev):
        return pltpu.make_async_remote_copy(
            src_ref=src, dst_ref=dst, send_sem=ss, recv_sem=rs, device_id=dev, device_id_type=MESH
        )

    def pb_dev(i):
        return {"pb": lax.rem(p + i, n_pb)}

    def ha_dev(i):
        return {"ha": lax.rem(h + i + n_ha, n_ha)}

    def ka_dev(i):
        return {"ka": lax.rem(k + i, n_ka)}

    def kcopy(head, slot):
        return pltpu.make_async_copy(kt_ref.at[head], kbuf.at[slot], ksem.at[slot])

    for n in range(NBUF):
        kcopy(n, n).start()

    barrier = pltpu.get_barrier_semaphore()
    for i in range(1, n_ha):
        pl.semaphore_signal(barrier, inc=1, device_id=ha_dev(i), device_id_type=MESH)
    for i in range(1, n_pb):
        pl.semaphore_signal(barrier, inc=1, device_id=pb_dev(i), device_id_type=MESH)
    for i in range(1, n_ka):
        pl.semaphore_signal(barrier, inc=1, device_id=ka_dev(i), device_id_type=MESH)
    def iq_copy(i):
        dest = lax.rem(h + i, n_ha)
        return copy_to(
            iq_ref.at[:, pl.ds(pl.multiple_of(dest * 64, 64), 64), :],
            iq_all.at[:, pl.ds(pl.multiple_of(h * 64, 64), 64), :],
            iq_s.at[i], iq_r.at[i], ha_dev(i),
        )

    def wc_copy(i):
        dest = lax.rem(h + i, n_ha)
        return copy_to(wc_ref.at[dest], wc_all.at[h], wc_s.at[i], wc_r.at[i], ha_dev(i))

    def cx_copy(i):
        return copy_to(
            ik_ref, ctx.at[pl.ds(pl.multiple_of(p * 256, 256), 256), :], cx_s.at[i], cx_r.at[i], pb_dev(i)
        )

    def greet():
        pl.semaphore_wait(barrier, n_ha + n_pb + n_ka - 3)
        for i in range(1, n_pb):
            cx_copy(i).start()
        for i in range(1, n_ha):
            iq_copy(i).start()
            wc_copy(i).start()

    lane = lax.broadcasted_iota(jnp.int32, (8, LANES), 1)
    for ref in (stm, stl):
        ref[...] = jnp.zeros_like(ref)
    first_key = k * keys

    def dest_of(i):
        return lax.rem(h + offsets[i] + n_ha, n_ha)

    for i in range(n_ha):
        pos_ref[i] = lane_spread(wc_ref[dest_of(i), 2:3, :])[0:32].astype(jnp.int32)

    def order_queries(head, carry):
        q_wide[...] = jnp.transpose(qt_ref[head].astype(jnp.float32), (1, 0))
        for i in range(n_ha):
            chunk = [
                q_wide[pl.ds(pl.multiple_of(kk * n_ha * 8 + dest_of(i) * 8, 8), 8), :] for kk in range(n_ka)
            ]
            q_ref[head, i * 32 : i * 32 + 32, :] = jnp.concatenate(chunk, axis=0).astype(jnp.bfloat16)
        return carry

    lax.fori_loop(0, heads, order_queries, 0)

    def scores(st, head, slot, out):
        lo, hi = spans[st]
        q = q_ref[head, lo * 32 : hi * 32, :]
        out[0 : (hi - lo) * 32] = jnp.dot(q, kbuf[slot], preferred_element_type=jnp.float32)

    def eslot(st, head):
        return lax.rem(st * heads + head, slots) if not isinstance(head, int) else (st * heads + head) % slots

    def soften(st, head, src):
        slot = eslot(st, head)
        lo, hi = spans[st]
        rows = (hi - lo) * 32
        span = slice(lo * 32, hi * 32)
        tops, sums = [], []
        for g in range(rows // 8):
            rel = pos_ref[lo + g // 4, (g % 4) * 8 : (g % 4) * 8 + 8, :] - first_key - lane
            x = [
                jnp.where(rel >= c * LANES, src[g * 8 : g * 8 + 8, c * LANES : (c + 1) * LANES], LOW)
                for c in range(tiles)
            ]
            top = functools.reduce(jnp.maximum, x)
            total = None
            for c in range(tiles):
                e = jnp.exp2((x[c] - top) * scale_main)
                e_ref[slot, g * 8 : g * 8 + 8, c * LANES : (c + 1) * LANES] = e
                total = e if total is None else total + e
            tops.append(top)
            sums.append(total)
        tops = jnp.concatenate(tops, axis=0)
        sums = jnp.concatenate(sums, axis=0)
        f_ref[head, span] = tops
        row_top = jnp.max(tops, axis=1, keepdims=True)
        row_sum = jnp.sum(sums * jnp.exp2((tops - row_top) * scale_main), axis=1, keepdims=True)
        here = lax.broadcasted_iota(jnp.int32, (rows, LANES), 1) == head
        stm[span] = jnp.where(here, row_top, stm[span])
        stl[span] = jnp.where(here, row_sum, stl[span])

    def st_copy(st, i):
        return copy_to(st_tx.at[st], st_rx.at[st, i], st_s.at[st, i], st_r.at[st, i], ka_dev(i))

    def send_stats(st):
        st_tx[st, 0:heads] = jnp.transpose(stm[...], (1, 0))[0:heads]
        st_tx[st, heads : 2 * heads] = jnp.transpose(stl[...], (1, 0))[0:heads]
        for i in range(1, n_ka):
            st_copy(st, i).start()

    def finish(st):
        for i in range(1, n_ka):
            st_copy(st, i).wait_recv()
        tops = [st_tx[st, 0:heads]] + [st_rx[st, i, 0:heads] for i in range(1, n_ka)]
        sums = [st_tx[st, heads : 2 * heads]] + [st_rx[st, i, heads : 2 * heads] for i in range(1, n_ka)]
        top = functools.reduce(jnp.maximum, tops)
        total = functools.reduce(
            jnp.add, [b * jnp.exp2((a - top) * scale_main) for a, b in zip(tops, sums)]
        )
        comb[0:heads] = top
        comb[heads : 2 * heads] = 1.0 / (total * main_total)
        lo, hi = spans[st]
        rows = (hi - lo) * 32
        span = slice(lo * 32, hi * 32)
        cols = jnp.transpose(comb[...], (1, 0))[span]
        for head in range(heads):
            gtop = jnp.broadcast_to(cols[:, head : head + 1], (rows, LANES))
            ginv = jnp.broadcast_to(cols[:, heads + head : heads + head + 1], (rows, LANES))
            f_ref[head, span] = jnp.exp2((f_ref[head, span] - gtop) * scale_main) * ginv

        def one(g, carry):
            at = pl.ds(pl.multiple_of(g * 8, 8), 8)
            acc = [jnp.zeros((8, LANES), jnp.float32) for _ in range(tiles)]
            for head in range(heads):
                f = f_ref[head, pl.ds(pl.multiple_of(lo * 32 + g * 8, 8), 8), :]
                slot = eslot(st, head)
                for c in range(tiles):
                    acc[c] = acc[c] + f * e_ref[slot, at, c * LANES : (c + 1) * LANES]
            spot = lo + g // 4
            to = pl.ds(pl.multiple_of(lax.rem(g, 4) * 8, 8), 8)
            for c in range(tiles):
                part, inner = divmod(c, tiles // 2)
                t_ref[spot, part, to, inner * LANES : (inner + 1) * LANES] = acc[c]
            return carry

        lax.fori_loop(0, rows // 8, one, 0)

    def spot_of(offset):
        return offsets.index(offset)

    def ra_copy(a, c):
        src = t_ref.at[spot_of(half if a == 0 else -(half - a)), c]
        return copy_to(src, rxa.at[a, c], ra_s.at[a, c], ra_r.at[a, c], ha_dev(-1))

    def rb_copy(a, c):
        src = t_ref.at[spot_of(half - a), c]
        return copy_to(src, rxb.at[a, c], rb_s.at[a, c], rb_r.at[a, c], ha_dev(1))

    def chain_a(a, c):
        if a > 1 or (a == 1 and c == 0):
            ra_copy(a - 1, c).wait_recv()
            spot = spot_of(-(half - a))
            t_ref[spot, c] = t_ref[spot, c] + rxa[a - 1, c]
        ra_copy(a, c).start()

    def chain_b(a, c):
        if a > 1 or (a == 1 and c == 1):
            rb_copy(a - 1, c).wait_recv()
            spot = spot_of(half - a)
            t_ref[spot, c] = t_ref[spot, c] + rxb[a - 1, c]
        rb_copy(a, c).start()

    def fwd(st, after, early):
        last = st == len(spans) - 1
        kcopy(0, 0).wait()
        scores(st, 0, 0, s0)
        kcopy(NBUF, 0).start()

        def pair(i, carry):
            h0 = 2 * i
            a = lax.rem(h0 + 1, NBUF)
            b = lax.rem(h0 + 2, NBUF)
            kcopy(h0 + 1, a).wait()
            kcopy(h0 + 2, b).wait()
            scores(st, h0 + 1, a, s1)
            soften(st, h0, s0)
            scores(st, h0 + 2, b, s0)
            soften(st, h0 + 1, s1)

            def refill():
                kcopy(lax.rem(h0 + 1 + NBUF, heads), a).start()
                kcopy(lax.rem(h0 + 2 + NBUF, heads), b).start()

            if last:
                pl.when(h0 + 1 + NBUF < heads)(lambda: kcopy(h0 + 1 + NBUF, a).start())
                pl.when(h0 + 2 + NBUF < heads)(lambda: kcopy(h0 + 2 + NBUF, b).start())
            else:
                refill()
            after(i)
            return carry

        if early is None:
            lax.fori_loop(0, heads // 2 - 1, pair, 0)
        else:
            lax.fori_loop(0, 1, pair, 0)
            early()
            lax.fori_loop(1, heads // 2 - 1, pair, 0)
        end = (heads - 1) % NBUF
        kcopy(heads - 1, end).wait()
        scores(st, heads - 1, end, s1)
        if not last:
            kcopy(NBUF - 1, end).start()
        soften(st, heads - 2, s0)
        soften(st, heads - 1, s1)

    fwd(0, lambda i: None, greet)
    send_stats(0)

    def beside(i):
        @pl.when(i == EXTRA // 2 - 1)
        def _():
            finish(0)
            chain_a(0, 0)
            chain_b(0, 1)
            chain_a(1, 1)
            chain_b(1, 0)

    def beside_last(i):
        @pl.when(i == 1)
        def _():
            chain_a(1, 0)
            chain_b(1, 1)

        @pl.when(i == EXTRA // 2 - 1)
        def _():
            finish(1)

    fwd(1, beside, None)
    send_stats(1)
    fwd(2, beside_last, None)
    send_stats(2)

    iq_all[:, pl.ds(pl.multiple_of(h * 64, 64), 64), :] = iq_ref[:, pl.ds(pl.multiple_of(h * 64, 64), 64), :]
    wc_all[h] = wc_ref[h]
    ctx[pl.ds(pl.multiple_of(p * 256, 256), 256), :] = ik_ref[...]
    for i in range(1, n_pb):
        cx_copy(i).wait_recv()
    for i in range(1, n_ha):
        iq_copy(i).wait_recv()
        wc_copy(i).wait_recv()
    ctx_t[...] = jnp.transpose(ctx[...].astype(jnp.float32), (1, 0)).astype(jnp.bfloat16)
    for src in range(n_ha):
        for kk in range(n_ka // 2):
            spread = lane_spread(wc_all[src, kk : kk + 1, :])
            for one in range(2):
                w_rep[2 * kk + one, src * 64 : src * 64 + 64, :] = spread[one * 64 : one * 64 + 64]
        spread = lane_spread(wc_ref[src, pl.ds(k // 2, 1), :])
        w_own[src * 64 : src * 64 + 64, :] = jnp.where(lax.rem(k, 2) == 0, spread[0:64], spread[64:128])
    per = n_ha * 64
    for kk in range(n_ka):
        wq = jnp.transpose(w_rep[kk] * iq_all[kk].astype(jnp.float32), (1, 0))
        big = wq.astype(jnp.bfloat16)
        wq_t[0:128, kk * per : (kk + 1) * per] = big
        wq_t[128:256, kk * per : (kk + 1) * per] = (wq - big.astype(jnp.float32)).astype(jnp.bfloat16)

    step = 512

    def index_part(n, carry):
        kk, sc = n // (keys // step), lax.rem(n, keys // step)
        at = pl.ds(pl.multiple_of(sc * step, step), step)
        act = jnp.dot(iq_all[kk], ctx_t[:, at], preferred_element_type=jnp.float32)
        w = w_rep[kk]
        parts = []
        for c in range(step // LANES):
            a = act[:, c * LANES : (c + 1) * LANES]
            r = jnp.maximum(a, 0.0) * w
            parts.append(jnp.sum(jnp.sum(r.reshape(n_ha, 64, LANES), axis=0).reshape(8, 8, LANES), axis=1))
        lg[kk, :, at] = jnp.concatenate(parts, axis=1) * scale
        m_ref[kk, :, at] = jnp.where(act > 0, 1.0, 0.0).astype(jnp.bfloat16)
        return carry

    total_parts = n_ka * (keys // step)
    for c in (1, 0):
        chain_a(2, c)
        chain_b(2, 1 - c)
    lax.fori_loop(0, total_parts, index_part, 0)

    rel = pos_ref[n_ha - 1][:, 0:1] - first_key
    seen = lax.broadcasted_iota(jnp.int32, (32, keys), 1) <= rel
    logits = jnp.where(seen, lg[...].reshape(32, keys), LOW)
    row_top = jnp.max(logits, axis=1, keepdims=True)
    expo = jnp.where(seen, jnp.exp(logits - row_top), 0.0)
    row_sum = jnp.sum(expo, axis=1, keepdims=True)
    lg[...] = expo.reshape(n_ka, 8, keys)
    ix_tx[0] = jnp.broadcast_to(row_top, (32, LANES))
    ix_tx[1] = jnp.broadcast_to(row_sum, (32, LANES))

    def ix_copy(i):
        return copy_to(ix_tx, ix_rx.at[i], ix_s.at[i], ix_r.at[i], ka_dev(i))

    for i in range(1, n_ka):
        ix_copy(i).start()
    finish(2)
    for c in range(2):
        chain_a(3, c)
        chain_b(3, c)
    for i in range(1, n_ka):
        ix_copy(i).wait_recv()
    tops = [ix_tx[0]] + [ix_rx[i, 0] for i in range(1, n_ka)]
    sums = [ix_tx[1]] + [ix_rx[i, 1] for i in range(1, n_ka)]
    top = functools.reduce(jnp.maximum, tops)
    total = functools.reduce(jnp.add, [b * jnp.exp(a - top) for a, b in zip(tops, sums)])
    factor = (jnp.exp(tops[0] - top) / total)[:, 0:1]

    def diff_half(c):
        ra_copy(half - 1, c).wait_recv()
        rb_copy(half - 1, c).wait_recv()
        at = slice(c * (keys // 2), (c + 1) * (keys // 2))
        target = t_ref[n_ha - 1, c] + rxa[half - 1, c] + rxb[half - 1, c]
        diff = (lg[:, :, at].reshape(32, keys // 2) * factor - target) * (key_total / 16.0)
        big = diff.astype(jnp.bfloat16).astype(jnp.float32)
        small = diff - big
        for t in range(32):
            kk, r = divmod(t, 8)
            if r % 2:
                continue
            for value, ref in ((big, d_hi), (small, d_lo)):
                both = jnp.concatenate(
                    [
                        jnp.broadcast_to(value[t : t + 1], (8, keys // 2)),
                        jnp.broadcast_to(value[t + 1 : t + 2], (8, keys // 2)),
                    ],
                    axis=0,
                )
                ref[kk, r * 8 : r * 8 + 16, at] = both.astype(jnp.bfloat16)

    def gk_copy(i):
        return copy_to(gk_tx.at[i], gk_rx.at[i], gk_s.at[i], gk_r.at[i], pb_dev(i))

    def gated(kk, at, width, d_ref):
        return (m_ref[kk, :, at].reshape(n_ha, 64, width) * d_ref[kk, :, at][None]).reshape(per, width)

    def key_block(n, carry):
        dest = (n // many) * many + lax.rem(p + n, many)
        i = lax.rem(dest - p + n_pb, n_pb)
        at = pl.ds(pl.multiple_of(dest * 256, 256), 256)
        wide = jnp.zeros((256, 256), jnp.float32)
        thin = jnp.zeros((128, 256), jnp.float32)
        for kk in range(n_ka):
            hi = gated(kk, at, 256, d_hi)
            lo = gated(kk, at, 256, d_lo)
            wide += jnp.dot(wq_t[:, kk * per : (kk + 1) * per], hi, preferred_element_type=jnp.float32)
            thin += jnp.dot(wq_t[0:128, kk * per : (kk + 1) * per], lo, preferred_element_type=jnp.float32)
        block = (wide[0:128] + wide[128:256] + thin) * scale
        gk_tx[i] = jnp.transpose(block, (1, 0))

        @pl.when(i > 0)
        def _():
            gk_copy(i).start()

        return carry

    many = n_pb // 2
    for c in range(2):
        diff_half(c)
        lax.fori_loop(c * many, (c + 1) * many, key_block, 0)

    core, far = lax.rem(k, 2), k // 2

    def query_rows(part, kk):
        mask = jnp.concatenate(
            [m_ref[kk, src * 64 + part * 32 : src * 64 + part * 32 + 32, :] for src in range(n_ha)], axis=0
        ).reshape(n_ha, 32, keys)
        hi = (mask * d_hi[kk, part * 32 : part * 32 + 32, :][None]).reshape(n_ha * 32, keys)
        lo = (mask * d_lo[kk, part * 32 : part * 32 + 32, :][None]).reshape(n_ha * 32, keys)
        key = ctx[...]
        u_ref[part, kk] = jnp.dot(hi, key, preferred_element_type=jnp.float32) + jnp.dot(
            lo, key, preferred_element_type=jnp.float32
        )

    def u_copy(part, x):
        return copy_to(
            u_ref.at[part, x * 2 + 1 - core], u_rx.at[part, x], u_s.at[part, x], u_r.at[part, x],
            {"ka": far * 2 + 1 - core},
        )

    def v_copy(part):
        return copy_to(
            v_ref.at[part, 1 - far], v_rx.at[part], v_s.at[part], v_r.at[part], {"ka": (1 - far) * 2 + core}
        )

    def o_copy(part, i):
        dest = lax.rem(h + i, n_ha)
        return copy_to(
            r_ref.at[part, pl.ds(pl.multiple_of(dest * 32, 32), 32), :],
            o_rx.at[h, part * 32 : part * 32 + 32, :],
            o_s.at[part, i], o_r.at[part, i], ha_dev(i),
        )

    def z_copy(i):
        return copy_to(z_tx.at[lax.rem(h + i, n_ha)], z_rx.at[i], z_s.at[i], z_r.at[i], ha_dev(i))

    def y_copy(i):
        return copy_to(zsum.at[h], zsum.at[h], y_s.at[i], y_r.at[i], ha_dev(i))

    def other_core(part, x):
        query_rows(part, x * 2 + 1 - core)
        u_copy(part, x).start()

    def own_core(part, x):
        query_rows(part, x * 2 + core)
        u_copy(part, x).wait_recv()
        v_ref[part, x] = u_ref[part, x * 2 + core] + u_rx[part, x]

    def to_owners(part):
        v_copy(part).wait_recv()
        r_ref[part] = (v_ref[part, far] + v_rx[part]) * scale
        for i in range(1, n_ha):
            o_copy(part, i).start()
        o_rx[h, part * 32 : part * 32 + 32, :] = r_ref[part, pl.ds(pl.multiple_of(h * 32, 32), 32), :]

    for part in range(2):
        other_core(part, 1 - far)
        own_core(part, 1 - far)
        v_copy(part).start()
    for part in range(2):
        other_core(part, far)
        own_core(part, far)
        to_owners(part)

    own = gk_tx[0]
    for i in range(1, n_pb):
        gk_copy(i).wait_recv()
        own = own + gk_rx[i]
    z_tx[...] = own.reshape(n_ha, 256 // n_ha, 128)
    for i in range(1, n_ha):
        z_copy(i).start()
    mine = z_tx[h]
    for i in range(1, n_ha):
        z_copy(i).wait_recv()
        mine = mine + z_rx[i]
    zsum[h] = mine
    for i in range(1, n_ha):
        y_copy(i).start()

    for part in range(2):
        for i in range(1, n_ha):
            o_copy(part, i).wait_recv()
    weight_sums = jnp.zeros((8, 64), jnp.float32)
    for b in range(4):
        at = slice(b * LANES, (b + 1) * LANES)
        u = o_rx[2 * b : 2 * b + 2].reshape(LANES, 128)
        gq_ref[at, :] = u * w_own[at, :]
        dots = jnp.transpose(u * iq_ref[k, at, :].astype(jnp.float32), (1, 0))
        sums = jnp.broadcast_to(jnp.sum(dots, axis=0, keepdims=True), (8, LANES))
        sums = jnp.where(lax.rem(lane, 8) == lax.broadcasted_iota(jnp.int32, (8, LANES), 0), sums, 0.0)
        row = lax.broadcasted_iota(jnp.int32, (LANES, 64), 0) // 8 + b * (LANES // 8)
        pick = jnp.where(row == lax.broadcasted_iota(jnp.int32, (LANES, 64), 1), 1.0, 0.0)
        weight_sums = weight_sums + jnp.dot(
            sums, pick, precision=lax.Precision.HIGHEST, preferred_element_type=jnp.float32
        )
    gw_ref[...] = weight_sums

    for i in range(1, n_ha):
        y_copy(i).wait_recv()
    gk_ref[...] = zsum[...].reshape(256, 128)

    for i in range(1, n_pb):
        cx_copy(i).wait_send()
        gk_copy(i).wait_send()
    for i in range(1, n_ha):
        iq_copy(i).wait_send()
        wc_copy(i).wait_send()
        z_copy(i).wait_send()
        for part in range(2):
            o_copy(part, i).wait_send()
        y_copy(i).wait_send()
    for i in range(1, n_ka):
        for st in range(len(spans)):
            st_copy(st, i).wait_send()
        ix_copy(i).wait_send()
    for a in range(half):
        for c in range(2):
            if a or c == 0:
                ra_copy(a, c).wait_send()
            if a or c == 1:
                rb_copy(a, c).wait_send()
    for part in range(2):
        for x in range(2):
            u_copy(part, x).wait_send()
        v_copy(part).wait_send()


def hand_over(gq_in, gw_in, gk_in, gq_out, gw_out, gk_out, sems):
    pairs = ((gq_in, gq_out), (gw_in, gw_out), (gk_in, gk_out))
    copies = [pltpu.make_async_copy(a, b, sems.at[n]) for n, (a, b) in enumerate(pairs)]
    for copy in copies:
        copy.start()
    for copy in copies:
        copy.wait()


def body(sizes, main_query, main_key, index_query, index_weight, index_key, query_pos):
    n_pb, n_ha, n_ka = sizes
    t, heads, dh = main_query.shape
    keys = main_key.shape[0]
    joined = index_query.shape[1]
    dims = (n_pb, n_ha, n_ka, heads, dh, keys, heads * n_ha, keys * n_ka)
    qt = main_query.transpose(1, 2, 0)
    kt = main_key.transpose(1, 2, 0)
    iq = index_query.reshape(n_ka, n_ha * 64, 128)
    wc = index_weight.astype(jnp.float32).reshape(n_ka, n_ha, 64).transpose(1, 0, 2)
    wc = wc.reshape(n_ha, n_ka * 64 // LANES, LANES)
    pos = query_pos.astype(jnp.float32).reshape(n_ka, n_ha, 8).transpose(1, 0, 2).reshape(n_ha, 1, 32)
    pos = jnp.pad(pos, ((0, 0), (0, 7 - wc.shape[1]), (0, LANES - 32)))
    wc = jnp.concatenate([wc, pos], axis=1)

    half = n_ha // 2
    firsts, rows = stages(n_ha)
    n_st = len(firsts) - 1
    per = n_ha * 64
    f32, bf16 = jnp.float32, jnp.bfloat16
    scratch = [
        pltpu.VMEM((heads, t, dh), bf16),
        pltpu.VMEM((t, dh), f32),
        pltpu.VMEM((n_ha, 32, LANES), jnp.int32),
        pltpu.VMEM((per, LANES), f32),
        pltpu.VMEM((NBUF, dh, keys), bf16),
        pltpu.VMEM((rows, keys), f32),
        pltpu.VMEM((rows, keys), f32),
        pltpu.VMEM((heads + EXTRA, rows, keys), f32),
        pltpu.VMEM((heads, t, LANES), f32),
        pltpu.VMEM((t, LANES), f32),
        pltpu.VMEM((t, LANES), f32),
        pltpu.VMEM((n_st, 2 * heads, t), f32),
        pltpu.VMEM((n_st, n_ka, 2 * heads, t), f32),
        pltpu.VMEM((LANES, t), f32),
        pltpu.VMEM((n_ha, 2, 32, keys // 2), f32),
        pltpu.VMEM((half, 2, 32, keys // 2), f32),
        pltpu.VMEM((half, 2, 32, keys // 2), f32),
        pltpu.VMEM((n_ka, per, 128), bf16),
        pltpu.VMEM((n_ha, 8, LANES), f32),
        pltpu.VMEM((n_ka, per, LANES), f32),
        pltpu.VMEM((256, n_ka * per), bf16),
        pltpu.VMEM((keys, 128), bf16),
        pltpu.VMEM((128, keys), bf16),
        pltpu.VMEM((n_ka, per, keys), bf16),
        pltpu.VMEM((n_ka, 8, keys), f32),
        pltpu.VMEM((n_ka, 64, keys), bf16),
        pltpu.VMEM((n_ka, 64, keys), bf16),
        pltpu.VMEM((2, 32, LANES), f32),
        pltpu.VMEM((n_ka, 2, 32, LANES), f32),
        pltpu.VMEM((2, n_ka, per // 2, 128), f32),
        pltpu.VMEM((2, 2, per // 2, 128), f32),
        pltpu.VMEM((2, 2, per // 2, 128), f32),
        pltpu.VMEM((2, per // 2, 128), f32),
        pltpu.VMEM((2, per // 2, 128), f32),
        pltpu.VMEM((n_ha, 64, 128), f32),
        pltpu.VMEM((n_pb, 256, 128), f32),
        pltpu.VMEM((n_pb, 256, 128), f32),
        pltpu.VMEM((n_ha, 256 // n_ha, 128), f32),
        pltpu.VMEM((n_ha, 256 // n_ha, 128), f32),
        pltpu.VMEM((n_ha, 256 // n_ha, 128), f32),
    ]
    dma = pltpu.SemaphoreType.DMA
    sems = [dma((NBUF,))]
    for shape in (
        (n_st, n_ka), (half, 2), (half, 2), (n_ha,), (n_ha,), (n_pb,),
        (n_ka,), (2, 2), (2,), (2, n_ha), (n_pb,), (n_ha,), (n_ha,),
    ):
        sems += [dma(shape), dma(shape)]
    vmem = pl.BlockSpec(memory_space=pltpu.VMEM)
    gq, gw, gk = pl.pallas_call(
        functools.partial(kernel, dims),
        out_shape=(
            jax.ShapeDtypeStruct((per, 128), f32),
            jax.ShapeDtypeStruct((8, 64), f32),
            jax.ShapeDtypeStruct((256, 128), f32),
        ),
        in_specs=[vmem, pl.BlockSpec(memory_space=pl.ANY)] + [vmem] * 3,
        out_specs=(vmem, vmem, vmem),
        scratch_shapes=scratch + sems,
        compiler_params=pltpu.CompilerParams(
            collective_id=0, has_side_effects=True, vmem_limit_bytes=63 * 1024 * 1024
        ),
    )(qt, kt, iq, wc, index_key)
    hbm = pl.BlockSpec(memory_space=pl.ANY)
    gq, gw, gk = pl.pallas_call(
        hand_over,
        out_shape=tuple(jax.ShapeDtypeStruct(x.shape, f32) for x in (gq, gw, gk)),
        in_specs=[hbm] * 3,
        out_specs=(hbm,) * 3,
        scratch_shapes=[dma((3,))],
    )(gq, gw, gk)
    return (gq.reshape(t // n_ka, joined, 128), gw.T, gk)


def solution(mesh):
    placed = (
        P("pb", "ha", None),
        P("ka", "ha", None),
        P("pb", "ha", None),
        P("pb", "ha"),
        P(("pb", "ka"), None),
        P("pb"),
    )
    sizes = tuple(mesh.shape[name] for name in ("pb", "ha", "ka"))
    return jax.shard_map(
        functools.partial(body, sizes),
        mesh=mesh,
        in_specs=placed,
        out_specs=(P(("pb", "ka"), "ha", None), P(("pb", "ka"), "ha"), P(("pb", "ka"), None)),
        check_vma=False,
    )
```

```python
import functools
import math

import jax
import jax.numpy as jnp
from jax import lax
from jax.experimental import pallas as pl
from jax.experimental.pallas import tpu as pltpu
from jax.sharding import PartitionSpec as P

MESH = pl.DeviceIdType.MESH
LOW = -1e30
LANES = 128
NBUF = 4
EXTRA = 6
LOG2E = 1.4426950408889634


def stages(n_ha):
    half = n_ha // 2
    firsts = (0, half - 1, half + 1, n_ha)
    return firsts, 32 * max(b - a for a, b in zip(firsts, firsts[1:]))


def lane_spread(row):
    return jnp.transpose(jnp.broadcast_to(row, (LANES, LANES)), (1, 0))


def kernel(
    dims,
    qt_ref, kt_ref, iq_ref, wc_ref, ik_ref,
    gq_ref, gw_ref, gk_ref,
    q_ref, q_wide, pos_ref, w_own, kbuf, s0, s1, e_ref, f_ref, stm, stl, st_tx, st_rx, comb,
    t_ref, rxa, rxb,
    iq_all, wc_all, w_rep, wq_t, ctx, ctx_t, m_ref, lg, d_hi, d_lo,
    ix_tx, ix_rx,
    u_ref, u_rx, v_ref, v_rx, r_ref, o_rx,
    gk_tx, gk_rx, z_tx, z_rx, zsum,
    ksem, st_s, st_r, ra_s, ra_r, rb_s, rb_r, iq_s, iq_r, wc_s, wc_r, cx_s, cx_r,
    ix_s, ix_r, u_s, u_r, v_s, v_r, o_s, o_r, gk_s, gk_r, z_s, z_r, y_s, y_r,
):
    n_pb, n_ha, n_ka, heads, dh, keys, main_total, key_total = dims
    p, h, k = lax.axis_index("pb"), lax.axis_index("ha"), lax.axis_index("ka")
    half = n_ha // 2
    firsts, most = stages(n_ha)
    spans = [(firsts[st], firsts[st + 1]) for st in range(len(firsts) - 1)]
    tiles = keys // LANES
    slots = heads + EXTRA
    scale_main = LOG2E / math.sqrt(dh)
    scale = 1.0 / math.sqrt(128)

    offsets = [half]
    for o in range(half - 1, 0, -1):
        offsets += [-o, o]
    offsets += [0]

    def copy_to(src, dst, ss, rs, dev):
        return pltpu.make_async_remote_copy(
            src_ref=src, dst_ref=dst, send_sem=ss, recv_sem=rs, device_id=dev, device_id_type=MESH
        )

    def pb_dev(i):
        return {"pb": lax.rem(p + i, n_pb)}

    def ha_dev(i):
        return {"ha": lax.rem(h + i + n_ha, n_ha)}

    def ka_dev(i):
        return {"ka": lax.rem(k + i, n_ka)}

    def kcopy(head, slot):
        return pltpu.make_async_copy(kt_ref.at[head], kbuf.at[slot], ksem.at[slot])

    for n in range(NBUF):
        kcopy(n, n).start()

    barrier = pltpu.get_barrier_semaphore()
    for i in range(1, n_ha):
        pl.semaphore_signal(barrier, inc=1, device_id=ha_dev(i), device_id_type=MESH)
    for i in range(1, n_pb):
        pl.semaphore_signal(barrier, inc=1, device_id=pb_dev(i), device_id_type=MESH)
    for i in range(1, n_ka):
        pl.semaphore_signal(barrier, inc=1, device_id=ka_dev(i), device_id_type=MESH)
    def iq_copy(i):
        dest = lax.rem(h + i, n_ha)
        return copy_to(
            iq_ref.at[:, pl.ds(pl.multiple_of(dest * 64, 64), 64), :],
            iq_all.at[:, pl.ds(pl.multiple_of(h * 64, 64), 64), :],
            iq_s.at[i], iq_r.at[i], ha_dev(i),
        )

    def wc_copy(i):
        dest = lax.rem(h + i, n_ha)
        return copy_to(wc_ref.at[dest], wc_all.at[h], wc_s.at[i], wc_r.at[i], ha_dev(i))

    def cx_copy(i):
        return copy_to(
            ik_ref, ctx.at[pl.ds(pl.multiple_of(p * 256, 256), 256), :], cx_s.at[i], cx_r.at[i], pb_dev(i)
        )

    def greet():
        pl.semaphore_wait(barrier, n_ha + n_pb + n_ka - 3)
        for i in range(1, n_pb):
            cx_copy(i).start()
        for i in range(1, n_ha):
            iq_copy(i).start()
            wc_copy(i).start()

    lane = lax.broadcasted_iota(jnp.int32, (8, LANES), 1)
    for ref in (stm, stl):
        ref[...] = jnp.zeros_like(ref)
    first_key = k * keys

    def dest_of(i):
        return lax.rem(h + offsets[i] + n_ha, n_ha)

    for i in range(n_ha):
        pos_ref[i] = lane_spread(wc_ref[dest_of(i), 2:3, :])[0:32].astype(jnp.int32)

    def order_queries(head, carry):
        q_wide[...] = jnp.transpose(qt_ref[head].astype(jnp.float32), (1, 0))
        for i in range(n_ha):
            chunk = [
                q_wide[pl.ds(pl.multiple_of(kk * n_ha * 8 + dest_of(i) * 8, 8), 8), :] for kk in range(n_ka)
            ]
            q_ref[head, i * 32 : i * 32 + 32, :] = jnp.concatenate(chunk, axis=0).astype(jnp.bfloat16)
        return carry

    lax.fori_loop(0, heads, order_queries, 0)

    def scores(st, head, slot, out):
        lo, hi = spans[st]
        q = q_ref[head, lo * 32 : hi * 32, :]
        out[0 : (hi - lo) * 32] = jnp.dot(q, kbuf[slot], preferred_element_type=jnp.float32)

    def eslot(st, head):
        return lax.rem(st * heads + head, slots) if not isinstance(head, int) else (st * heads + head) % slots

    def soften(st, head, src):
        slot = eslot(st, head)
        lo, hi = spans[st]
        rows = (hi - lo) * 32
        span = slice(lo * 32, hi * 32)
        tops, sums = [], []
        for g in range(rows // 8):
            rel = pos_ref[lo + g // 4, (g % 4) * 8 : (g % 4) * 8 + 8, :] - first_key - lane
            x = [
                jnp.where(rel >= c * LANES, src[g * 8 : g * 8 + 8, c * LANES : (c + 1) * LANES], LOW)
                for c in range(tiles)
            ]
            top = functools.reduce(jnp.maximum, x)
            total = None
            for c in range(tiles):
                e = jnp.exp2((x[c] - top) * scale_main)
                e_ref[slot, g * 8 : g * 8 + 8, c * LANES : (c + 1) * LANES] = e
                total = e if total is None else total + e
            tops.append(top)
            sums.append(total)
        tops = jnp.concatenate(tops, axis=0)
        sums = jnp.concatenate(sums, axis=0)
        f_ref[head, span] = tops
        row_top = jnp.max(tops, axis=1, keepdims=True)
        row_sum = jnp.sum(sums * jnp.exp2((tops - row_top) * scale_main), axis=1, keepdims=True)
        here = lax.broadcasted_iota(jnp.int32, (rows, LANES), 1) == head
        stm[span] = jnp.where(here, row_top, stm[span])
        stl[span] = jnp.where(here, row_sum, stl[span])

    def st_copy(st, i):
        return copy_to(st_tx.at[st], st_rx.at[st, i], st_s.at[st, i], st_r.at[st, i], ka_dev(i))

    def send_stats(st):
        st_tx[st, 0:heads] = jnp.transpose(stm[...], (1, 0))[0:heads]
        st_tx[st, heads : 2 * heads] = jnp.transpose(stl[...], (1, 0))[0:heads]
        for i in range(1, n_ka):
            st_copy(st, i).start()

    def finish(st):
        for i in range(1, n_ka):
            st_copy(st, i).wait_recv()
        tops = [st_tx[st, 0:heads]] + [st_rx[st, i, 0:heads] for i in range(1, n_ka)]
        sums = [st_tx[st, heads : 2 * heads]] + [st_rx[st, i, heads : 2 * heads] for i in range(1, n_ka)]
        top = functools.reduce(jnp.maximum, tops)
        total = functools.reduce(
            jnp.add, [b * jnp.exp2((a - top) * scale_main) for a, b in zip(tops, sums)]
        )
        comb[0:heads] = top
        comb[heads : 2 * heads] = 1.0 / (total * main_total)
        lo, hi = spans[st]
        rows = (hi - lo) * 32
        span = slice(lo * 32, hi * 32)
        cols = jnp.transpose(comb[...], (1, 0))[span]
        for head in range(heads):
            gtop = jnp.broadcast_to(cols[:, head : head + 1], (rows, LANES))
            ginv = jnp.broadcast_to(cols[:, heads + head : heads + head + 1], (rows, LANES))
            f_ref[head, span] = jnp.exp2((f_ref[head, span] - gtop) * scale_main) * ginv

        def one(g, carry):
            at = pl.ds(pl.multiple_of(g * 8, 8), 8)
            acc = [jnp.zeros((8, LANES), jnp.float32) for _ in range(tiles)]
            for head in range(heads):
                f = f_ref[head, pl.ds(pl.multiple_of(lo * 32 + g * 8, 8), 8), :]
                slot = eslot(st, head)
                for c in range(tiles):
                    acc[c] = acc[c] + f * e_ref[slot, at, c * LANES : (c + 1) * LANES]
            spot = lo + g // 4
            to = pl.ds(pl.multiple_of(lax.rem(g, 4) * 8, 8), 8)
            for c in range(tiles):
                part, inner = divmod(c, tiles // 2)
                t_ref[spot, part, to, inner * LANES : (inner + 1) * LANES] = acc[c]
            return carry

        lax.fori_loop(0, rows // 8, one, 0)

    def spot_of(offset):
        return offsets.index(offset)

    def ra_copy(a, c):
        src = t_ref.at[spot_of(half if a == 0 else -(half - a)), c]
        return copy_to(src, rxa.at[a, c], ra_s.at[a, c], ra_r.at[a, c], ha_dev(-1))

    def rb_copy(a, c):
        src = t_ref.at[spot_of(half - a), c]
        return copy_to(src, rxb.at[a, c], rb_s.at[a, c], rb_r.at[a, c], ha_dev(1))

    def chain_a(a, c):
        if a > 1 or (a == 1 and c == 0):
            ra_copy(a - 1, c).wait_recv()
            spot = spot_of(-(half - a))
            t_ref[spot, c] = t_ref[spot, c] + rxa[a - 1, c]
        ra_copy(a, c).start()

    def chain_b(a, c):
        if a > 1 or (a == 1 and c == 1):
            rb_copy(a - 1, c).wait_recv()
            spot = spot_of(half - a)
            t_ref[spot, c] = t_ref[spot, c] + rxb[a - 1, c]
        rb_copy(a, c).start()

    def fwd(st, after, early):
        last = st == len(spans) - 1
        kcopy(0, 0).wait()
        scores(st, 0, 0, s0)
        kcopy(NBUF, 0).start()

        def pair(i, carry):
            h0 = 2 * i
            a = lax.rem(h0 + 1, NBUF)
            b = lax.rem(h0 + 2, NBUF)
            kcopy(h0 + 1, a).wait()
            kcopy(h0 + 2, b).wait()
            scores(st, h0 + 1, a, s1)
            soften(st, h0, s0)
            scores(st, h0 + 2, b, s0)
            soften(st, h0 + 1, s1)

            def refill():
                kcopy(lax.rem(h0 + 1 + NBUF, heads), a).start()
                kcopy(lax.rem(h0 + 2 + NBUF, heads), b).start()

            if last:
                pl.when(h0 + 1 + NBUF < heads)(lambda: kcopy(h0 + 1 + NBUF, a).start())
                pl.when(h0 + 2 + NBUF < heads)(lambda: kcopy(h0 + 2 + NBUF, b).start())
            else:
                refill()
            after(i)
            return carry

        if early is None:
            lax.fori_loop(0, heads // 2 - 1, pair, 0)
        else:
            lax.fori_loop(0, 1, pair, 0)
            early()
            lax.fori_loop(1, heads // 2 - 1, pair, 0)
        end = (heads - 1) % NBUF
        kcopy(heads - 1, end).wait()
        scores(st, heads - 1, end, s1)
        if not last:
            kcopy(NBUF - 1, end).start()
        soften(st, heads - 2, s0)
        soften(st, heads - 1, s1)

    fwd(0, lambda i: None, greet)
    send_stats(0)

    def beside(i):
        @pl.when(i == EXTRA // 2 - 1)
        def _():
            finish(0)
            chain_a(0, 0)
            chain_b(0, 1)
            chain_a(1, 1)
            chain_b(1, 0)

    def beside_last(i):
        @pl.when(i == 1)
        def _():
            chain_a(1, 0)
            chain_b(1, 1)

        @pl.when(i == EXTRA // 2 - 1)
        def _():
            finish(1)

    fwd(1, beside, None)
    send_stats(1)
    fwd(2, beside_last, None)
    send_stats(2)

    iq_all[:, pl.ds(pl.multiple_of(h * 64, 64), 64), :] = iq_ref[:, pl.ds(pl.multiple_of(h * 64, 64), 64), :]
    wc_all[h] = wc_ref[h]
    ctx[pl.ds(pl.multiple_of(p * 256, 256), 256), :] = ik_ref[...]
    for i in range(1, n_pb):
        cx_copy(i).wait_recv()
    for i in range(1, n_ha):
        iq_copy(i).wait_recv()
        wc_copy(i).wait_recv()
    ctx_t[...] = jnp.transpose(ctx[...].astype(jnp.float32), (1, 0)).astype(jnp.bfloat16)
    for src in range(n_ha):
        for kk in range(n_ka // 2):
            spread = lane_spread(wc_all[src, kk : kk + 1, :])
            for one in range(2):
                w_rep[2 * kk + one, src * 64 : src * 64 + 64, :] = spread[one * 64 : one * 64 + 64]
        spread = lane_spread(wc_ref[src, pl.ds(k // 2, 1), :])
        w_own[src * 64 : src * 64 + 64, :] = jnp.where(lax.rem(k, 2) == 0, spread[0:64], spread[64:128])
    per = n_ha * 64
    for kk in range(n_ka):
        wq = jnp.transpose(w_rep[kk] * iq_all[kk].astype(jnp.float32), (1, 0))
        big = wq.astype(jnp.bfloat16)
        wq_t[0:128, kk * per : (kk + 1) * per] = big
        wq_t[128:256, kk * per : (kk + 1) * per] = (wq - big.astype(jnp.float32)).astype(jnp.bfloat16)

    step = 512

    def index_part(n, carry):
        kk, sc = n // (keys // step), lax.rem(n, keys // step)
        at = pl.ds(pl.multiple_of(sc * step, step), step)
        act = jnp.dot(iq_all[kk], ctx_t[:, at], preferred_element_type=jnp.float32)
        w = w_rep[kk]
        parts = []
        for c in range(step // LANES):
            a = act[:, c * LANES : (c + 1) * LANES]
            r = jnp.maximum(a, 0.0) * w
            parts.append(jnp.sum(jnp.sum(r.reshape(n_ha, 64, LANES), axis=0).reshape(8, 8, LANES), axis=1))
        lg[kk, :, at] = jnp.concatenate(parts, axis=1) * scale
        m_ref[kk, :, at] = jnp.where(act > 0, 1.0, 0.0).astype(jnp.bfloat16)
        return carry

    total_parts = n_ka * (keys // step)
    for c in (1, 0):
        chain_a(2, c)
        chain_b(2, 1 - c)
    lax.fori_loop(0, total_parts, index_part, 0)

    rel = pos_ref[n_ha - 1][:, 0:1] - first_key
    seen = lax.broadcasted_iota(jnp.int32, (32, keys), 1) <= rel
    logits = jnp.where(seen, lg[...].reshape(32, keys), LOW)
    row_top = jnp.max(logits, axis=1, keepdims=True)
    expo = jnp.where(seen, jnp.exp(logits - row_top), 0.0)
    row_sum = jnp.sum(expo, axis=1, keepdims=True)
    lg[...] = expo.reshape(n_ka, 8, keys)
    ix_tx[0] = jnp.broadcast_to(row_top, (32, LANES))
    ix_tx[1] = jnp.broadcast_to(row_sum, (32, LANES))

    def ix_copy(i):
        return copy_to(ix_tx, ix_rx.at[i], ix_s.at[i], ix_r.at[i], ka_dev(i))

    for i in range(1, n_ka):
        ix_copy(i).start()
    finish(2)
    for c in range(2):
        chain_a(3, c)
        chain_b(3, c)
    for i in range(1, n_ka):
        ix_copy(i).wait_recv()
    tops = [ix_tx[0]] + [ix_rx[i, 0] for i in range(1, n_ka)]
    sums = [ix_tx[1]] + [ix_rx[i, 1] for i in range(1, n_ka)]
    top = functools.reduce(jnp.maximum, tops)
    total = functools.reduce(jnp.add, [b * jnp.exp(a - top) for a, b in zip(tops, sums)])
    factor = (jnp.exp(tops[0] - top) / total)[:, 0:1]

    def diff_half(c):
        ra_copy(half - 1, c).wait_recv()
        rb_copy(half - 1, c).wait_recv()
        at = slice(c * (keys // 2), (c + 1) * (keys // 2))
        target = t_ref[n_ha - 1, c] + rxa[half - 1, c] + rxb[half - 1, c]
        diff = (lg[:, :, at].reshape(32, keys // 2) * factor - target) * (key_total / 16.0)
        big = diff.astype(jnp.bfloat16).astype(jnp.float32)
        small = diff - big
        for t in range(32):
            kk, r = divmod(t, 8)
            if r % 2:
                continue
            for value, ref in ((big, d_hi), (small, d_lo)):
                both = jnp.concatenate(
                    [
                        jnp.broadcast_to(value[t : t + 1], (8, keys // 2)),
                        jnp.broadcast_to(value[t + 1 : t + 2], (8, keys // 2)),
                    ],
                    axis=0,
                )
                ref[kk, r * 8 : r * 8 + 16, at] = both.astype(jnp.bfloat16)

    def gk_copy(i):
        return copy_to(gk_tx.at[i], gk_rx.at[i], gk_s.at[i], gk_r.at[i], pb_dev(i))

    def gated(kk, at, width, d_ref):
        return (m_ref[kk, :, at].reshape(n_ha, 64, width) * d_ref[kk, :, at][None]).reshape(per, width)

    def key_block(n, carry):
        i = lax.rem(n + 1, n_pb)
        dest = lax.rem(p + n + 1, n_pb)
        at = pl.ds(pl.multiple_of(dest * 256, 256), 256)
        wide = jnp.zeros((256, 256), jnp.float32)
        thin = jnp.zeros((128, 256), jnp.float32)
        for kk in range(n_ka):
            hi = gated(kk, at, 256, d_hi)
            lo = gated(kk, at, 256, d_lo)
            wide += jnp.dot(wq_t[:, kk * per : (kk + 1) * per], hi, preferred_element_type=jnp.float32)
            thin += jnp.dot(wq_t[0:128, kk * per : (kk + 1) * per], lo, preferred_element_type=jnp.float32)
        block = (wide[0:128] + wide[128:256] + thin) * scale
        gk_tx[i] = jnp.transpose(block, (1, 0))

        @pl.when(i > 0)
        def _():
            gk_copy(i).start()

        return carry

    for c in range(2):
        diff_half(c)
    lax.fori_loop(0, n_pb, key_block, 0)

    core, far = lax.rem(k, 2), k // 2

    def query_rows(part, kk):
        mask = jnp.concatenate(
            [m_ref[kk, src * 64 + part * 32 : src * 64 + part * 32 + 32, :] for src in range(n_ha)], axis=0
        ).reshape(n_ha, 32, keys)
        hi = (mask * d_hi[kk, part * 32 : part * 32 + 32, :][None]).reshape(n_ha * 32, keys)
        lo = (mask * d_lo[kk, part * 32 : part * 32 + 32, :][None]).reshape(n_ha * 32, keys)
        key = ctx[...]
        u_ref[part, kk] = jnp.dot(hi, key, preferred_element_type=jnp.float32) + jnp.dot(
            lo, key, preferred_element_type=jnp.float32
        )

    def u_copy(part, x):
        return copy_to(
            u_ref.at[part, x * 2 + 1 - core], u_rx.at[part, x], u_s.at[part, x], u_r.at[part, x],
            {"ka": far * 2 + 1 - core},
        )

    def v_copy(part):
        return copy_to(
            v_ref.at[part, 1 - far], v_rx.at[part], v_s.at[part], v_r.at[part], {"ka": (1 - far) * 2 + core}
        )

    def o_copy(part, i):
        dest = lax.rem(h + i, n_ha)
        return copy_to(
            r_ref.at[part, pl.ds(pl.multiple_of(dest * 32, 32), 32), :],
            o_rx.at[h, part * 32 : part * 32 + 32, :],
            o_s.at[part, i], o_r.at[part, i], ha_dev(i),
        )

    def z_copy(i):
        return copy_to(z_tx.at[lax.rem(h + i, n_ha)], z_rx.at[i], z_s.at[i], z_r.at[i], ha_dev(i))

    def y_copy(i):
        return copy_to(zsum.at[h], zsum.at[h], y_s.at[i], y_r.at[i], ha_dev(i))

    def other_core(part, x):
        query_rows(part, x * 2 + 1 - core)
        u_copy(part, x).start()

    def own_core(part, x):
        query_rows(part, x * 2 + core)
        u_copy(part, x).wait_recv()
        v_ref[part, x] = u_ref[part, x * 2 + core] + u_rx[part, x]

    def to_owners(part):
        v_copy(part).wait_recv()
        r_ref[part] = (v_ref[part, far] + v_rx[part]) * scale
        for i in range(1, n_ha):
            o_copy(part, i).start()
        o_rx[h, part * 32 : part * 32 + 32, :] = r_ref[part, pl.ds(pl.multiple_of(h * 32, 32), 32), :]

    for part in range(2):
        other_core(part, 1 - far)
        own_core(part, 1 - far)
        v_copy(part).start()
    for part in range(2):
        other_core(part, far)
        own_core(part, far)
        if part == 0:
            to_owners(0)

    own = gk_tx[0]
    for i in range(1, n_pb):
        gk_copy(i).wait_recv()
        own = own + gk_rx[i]
    z_tx[...] = own.reshape(n_ha, 256 // n_ha, 128)
    for i in range(1, n_ha):
        z_copy(i).start()
    to_owners(1)
    mine = z_tx[h]
    for i in range(1, n_ha):
        z_copy(i).wait_recv()
        mine = mine + z_rx[i]
    zsum[h] = mine
    for i in range(1, n_ha):
        y_copy(i).start()

    for part in range(2):
        for i in range(1, n_ha):
            o_copy(part, i).wait_recv()
    weight_sums = jnp.zeros((8, 64), jnp.float32)
    for b in range(4):
        at = slice(b * LANES, (b + 1) * LANES)
        u = o_rx[2 * b : 2 * b + 2].reshape(LANES, 128)
        gq_ref[at, :] = u * w_own[at, :]
        dots = jnp.transpose(u * iq_ref[k, at, :].astype(jnp.float32), (1, 0))
        sums = jnp.broadcast_to(jnp.sum(dots, axis=0, keepdims=True), (8, LANES))
        sums = jnp.where(lax.rem(lane, 8) == lax.broadcasted_iota(jnp.int32, (8, LANES), 0), sums, 0.0)
        row = lax.broadcasted_iota(jnp.int32, (LANES, 64), 0) // 8 + b * (LANES // 8)
        pick = jnp.where(row == lax.broadcasted_iota(jnp.int32, (LANES, 64), 1), 1.0, 0.0)
        weight_sums = weight_sums + jnp.dot(
            sums, pick, precision=lax.Precision.HIGHEST, preferred_element_type=jnp.float32
        )
    gw_ref[...] = weight_sums

    for i in range(1, n_ha):
        y_copy(i).wait_recv()
    gk_ref[...] = zsum[...].reshape(256, 128)

    for i in range(1, n_pb):
        cx_copy(i).wait_send()
        gk_copy(i).wait_send()
    for i in range(1, n_ha):
        iq_copy(i).wait_send()
        wc_copy(i).wait_send()
        z_copy(i).wait_send()
        for part in range(2):
            o_copy(part, i).wait_send()
        y_copy(i).wait_send()
    for i in range(1, n_ka):
        for st in range(len(spans)):
            st_copy(st, i).wait_send()
        ix_copy(i).wait_send()
    for a in range(half):
        for c in range(2):
            if a or c == 0:
                ra_copy(a, c).wait_send()
            if a or c == 1:
                rb_copy(a, c).wait_send()
    for part in range(2):
        for x in range(2):
            u_copy(part, x).wait_send()
        v_copy(part).wait_send()


def body(sizes, main_query, main_key, index_query, index_weight, index_key, query_pos):
    n_pb, n_ha, n_ka = sizes
    t, heads, dh = main_query.shape
    keys = main_key.shape[0]
    joined = index_query.shape[1]
    dims = (n_pb, n_ha, n_ka, heads, dh, keys, heads * n_ha, keys * n_ka)
    qt = main_query.transpose(1, 2, 0)
    kt = main_key.transpose(1, 2, 0)
    iq = index_query.reshape(n_ka, n_ha * 64, 128)
    wc = index_weight.astype(jnp.float32).reshape(n_ka, n_ha, 64).transpose(1, 0, 2)
    wc = wc.reshape(n_ha, n_ka * 64 // LANES, LANES)
    pos = query_pos.astype(jnp.float32).reshape(n_ka, n_ha, 8).transpose(1, 0, 2).reshape(n_ha, 1, 32)
    pos = jnp.pad(pos, ((0, 0), (0, 7 - wc.shape[1]), (0, LANES - 32)))
    wc = jnp.concatenate([wc, pos], axis=1)

    half = n_ha // 2
    firsts, rows = stages(n_ha)
    n_st = len(firsts) - 1
    per = n_ha * 64
    f32, bf16 = jnp.float32, jnp.bfloat16
    scratch = [
        pltpu.VMEM((heads, t, dh), bf16),
        pltpu.VMEM((t, dh), f32),
        pltpu.VMEM((n_ha, 32, LANES), jnp.int32),
        pltpu.VMEM((per, LANES), f32),
        pltpu.VMEM((NBUF, dh, keys), bf16),
        pltpu.VMEM((rows, keys), f32),
        pltpu.VMEM((rows, keys), f32),
        pltpu.VMEM((heads + EXTRA, rows, keys), f32),
        pltpu.VMEM((heads, t, LANES), f32),
        pltpu.VMEM((t, LANES), f32),
        pltpu.VMEM((t, LANES), f32),
        pltpu.VMEM((n_st, 2 * heads, t), f32),
        pltpu.VMEM((n_st, n_ka, 2 * heads, t), f32),
        pltpu.VMEM((LANES, t), f32),
        pltpu.VMEM((n_ha, 2, 32, keys // 2), f32),
        pltpu.VMEM((half, 2, 32, keys // 2), f32),
        pltpu.VMEM((half, 2, 32, keys // 2), f32),
        pltpu.VMEM((n_ka, per, 128), bf16),
        pltpu.VMEM((n_ha, 8, LANES), f32),
        pltpu.VMEM((n_ka, per, LANES), f32),
        pltpu.VMEM((256, n_ka * per), bf16),
        pltpu.VMEM((keys, 128), bf16),
        pltpu.VMEM((128, keys), bf16),
        pltpu.VMEM((n_ka, per, keys), bf16),
        pltpu.VMEM((n_ka, 8, keys), f32),
        pltpu.VMEM((n_ka, 64, keys), bf16),
        pltpu.VMEM((n_ka, 64, keys), bf16),
        pltpu.VMEM((2, 32, LANES), f32),
        pltpu.VMEM((n_ka, 2, 32, LANES), f32),
        pltpu.VMEM((2, n_ka, per // 2, 128), f32),
        pltpu.VMEM((2, 2, per // 2, 128), f32),
        pltpu.VMEM((2, 2, per // 2, 128), f32),
        pltpu.VMEM((2, per // 2, 128), f32),
        pltpu.VMEM((2, per // 2, 128), f32),
        pltpu.VMEM((n_ha, 64, 128), f32),
        pltpu.VMEM((n_pb, 256, 128), f32),
        pltpu.VMEM((n_pb, 256, 128), f32),
        pltpu.VMEM((n_ha, 256 // n_ha, 128), f32),
        pltpu.VMEM((n_ha, 256 // n_ha, 128), f32),
        pltpu.VMEM((n_ha, 256 // n_ha, 128), f32),
    ]
    dma = pltpu.SemaphoreType.DMA
    sems = [dma((NBUF,))]
    for shape in (
        (n_st, n_ka), (half, 2), (half, 2), (n_ha,), (n_ha,), (n_pb,),
        (n_ka,), (2, 2), (2,), (2, n_ha), (n_pb,), (n_ha,), (n_ha,),
    ):
        sems += [dma(shape), dma(shape)]
    vmem = pl.BlockSpec(memory_space=pltpu.VMEM)
    gq, gw, gk = pl.pallas_call(
        functools.partial(kernel, dims),
        out_shape=(
            jax.ShapeDtypeStruct((per, 128), f32),
            jax.ShapeDtypeStruct((8, 64), f32),
            jax.ShapeDtypeStruct((256, 128), f32),
        ),
        in_specs=[vmem, pl.BlockSpec(memory_space=pl.ANY)] + [vmem] * 3,
        out_specs=(vmem, vmem, vmem),
        scratch_shapes=scratch + sems,
        compiler_params=pltpu.CompilerParams(
            collective_id=0, has_side_effects=True, vmem_limit_bytes=63 * 1024 * 1024
        ),
    )(qt, kt, iq, wc, index_key)
    return (gq.reshape(t // n_ka, joined, 128), gw.T, gk)


def solution(mesh):
    placed = (
        P("pb", "ha", None),
        P("ka", "ha", None),
        P("pb", "ha", None),
        P("pb", "ha"),
        P(("pb", "ka"), None),
        P("pb"),
    )
    sizes = tuple(mesh.shape[name] for name in ("pb", "ha", "ka"))
    return jax.shard_map(
        functools.partial(body, sizes),
        mesh=mesh,
        in_specs=placed,
        out_specs=(P(("pb", "ka"), "ha", None), P(("pb", "ka"), "ha"), P(("pb", "ka"), None)),
        check_vma=False,
    )
```

```python
import functools
import math

import jax
import jax.numpy as jnp
from jax import lax
from jax.experimental import pallas as pl
from jax.experimental.pallas import tpu as pltpu
from jax.sharding import PartitionSpec as P

MESH = pl.DeviceIdType.MESH
LOW = -1e30
LANES = 128
NBUF = 4
EXTRA = 6
LOG2E = 1.4426950408889634


def stages(n_ha):
    half = n_ha // 2
    firsts = (0, half - 1, half + 1, n_ha)
    return firsts, 32 * max(b - a for a, b in zip(firsts, firsts[1:]))


def lane_spread(row):
    return jnp.transpose(jnp.broadcast_to(row, (LANES, LANES)), (1, 0))


def kernel(
    dims,
    qt_ref, kt_ref, iq_ref, wc_ref, ik_ref,
    gq_ref, gw_ref, gk_ref,
    q_ref, q_wide, pos_ref, w_own, kbuf, s0, s1, e_ref, f_ref, stm, stl, st_tx, st_rx, comb,
    t_ref, rxa, rxb,
    iq_all, wc_all, w_rep, wq_t, ctx, ctx_t, m_ref, lg, d_hi, d_lo,
    ix_tx, ix_rx,
    u_ref, u_rx, v_ref, v_rx, r_ref, o_rx,
    gk_tx, gk_rx, z_tx, z_rx, zsum,
    ksem, st_s, st_r, ra_s, ra_r, rb_s, rb_r, iq_s, iq_r, wc_s, wc_r, cx_s, cx_r,
    ix_s, ix_r, u_s, u_r, v_s, v_r, o_s, o_r, gk_s, gk_r, z_s, z_r, y_s, y_r,
):
    n_pb, n_ha, n_ka, heads, dh, keys, main_total, key_total = dims
    p, h, k = lax.axis_index("pb"), lax.axis_index("ha"), lax.axis_index("ka")
    half = n_ha // 2
    firsts, most = stages(n_ha)
    spans = [(firsts[st], firsts[st + 1]) for st in range(len(firsts) - 1)]
    tiles = keys // LANES
    slots = heads + EXTRA
    scale_main = LOG2E / math.sqrt(dh)
    scale = 1.0 / math.sqrt(128)

    offsets = [half]
    for o in range(half - 1, 0, -1):
        offsets += [-o, o]
    offsets += [0]

    def copy_to(src, dst, ss, rs, dev):
        return pltpu.make_async_remote_copy(
            src_ref=src, dst_ref=dst, send_sem=ss, recv_sem=rs, device_id=dev, device_id_type=MESH
        )

    def pb_dev(i):
        return {"pb": lax.rem(p + i, n_pb)}

    def ha_dev(i):
        return {"ha": lax.rem(h + i + n_ha, n_ha)}

    def ka_dev(i):
        return {"ka": lax.rem(k + i, n_ka)}

    def kcopy(head, slot):
        return pltpu.make_async_copy(kt_ref.at[head], kbuf.at[slot], ksem.at[slot])

    for n in range(NBUF):
        kcopy(n, n).start()

    barrier = pltpu.get_barrier_semaphore()
    for i in range(1, n_ha):
        pl.semaphore_signal(barrier, inc=1, device_id=ha_dev(i), device_id_type=MESH)
    for i in range(1, n_pb):
        pl.semaphore_signal(barrier, inc=1, device_id=pb_dev(i), device_id_type=MESH)
    for i in range(1, n_ka):
        pl.semaphore_signal(barrier, inc=1, device_id=ka_dev(i), device_id_type=MESH)
    def iq_copy(i):
        dest = lax.rem(h + i, n_ha)
        return copy_to(
            iq_ref.at[:, pl.ds(pl.multiple_of(dest * 64, 64), 64), :],
            iq_all.at[:, pl.ds(pl.multiple_of(h * 64, 64), 64), :],
            iq_s.at[i], iq_r.at[i], ha_dev(i),
        )

    def wc_copy(i):
        dest = lax.rem(h + i, n_ha)
        return copy_to(wc_ref.at[dest], wc_all.at[h], wc_s.at[i], wc_r.at[i], ha_dev(i))

    def cx_copy(i):
        return copy_to(
            ik_ref, ctx.at[pl.ds(pl.multiple_of(p * 256, 256), 256), :], cx_s.at[i], cx_r.at[i], pb_dev(i)
        )

    def greet():
        pl.semaphore_wait(barrier, n_ha + n_pb + n_ka - 3)
        for i in range(1, n_pb):
            cx_copy(i).start()
        for i in range(1, n_ha):
            iq_copy(i).start()
            wc_copy(i).start()

    lane = lax.broadcasted_iota(jnp.int32, (8, LANES), 1)
    for ref in (stm, stl):
        ref[...] = jnp.zeros_like(ref)
    first_key = k * keys

    def dest_of(i):
        return lax.rem(h + offsets[i] + n_ha, n_ha)

    for i in range(n_ha):
        pos_ref[i] = lane_spread(wc_ref[dest_of(i), 2:3, :])[0:32].astype(jnp.int32)

    def order_queries(head, carry):
        q_wide[...] = jnp.transpose(qt_ref[head].astype(jnp.float32), (1, 0))
        for i in range(n_ha):
            chunk = [
                q_wide[pl.ds(pl.multiple_of(kk * n_ha * 8 + dest_of(i) * 8, 8), 8), :] for kk in range(n_ka)
            ]
            q_ref[head, i * 32 : i * 32 + 32, :] = jnp.concatenate(chunk, axis=0).astype(jnp.bfloat16)
        return carry

    lax.fori_loop(0, heads, order_queries, 0)

    def scores(st, head, slot, out):
        lo, hi = spans[st]
        q = q_ref[head, lo * 32 : hi * 32, :]
        out[0 : (hi - lo) * 32] = jnp.dot(q, kbuf[slot], preferred_element_type=jnp.float32)

    def eslot(st, head):
        return lax.rem(st * heads + head, slots) if not isinstance(head, int) else (st * heads + head) % slots

    def soften(st, head, src):
        slot = eslot(st, head)
        lo, hi = spans[st]
        rows = (hi - lo) * 32
        span = slice(lo * 32, hi * 32)
        tops, sums = [], []
        for g in range(rows // 8):
            rel = pos_ref[lo + g // 4, (g % 4) * 8 : (g % 4) * 8 + 8, :] - first_key - lane
            x = [
                jnp.where(rel >= c * LANES, src[g * 8 : g * 8 + 8, c * LANES : (c + 1) * LANES], LOW)
                for c in range(tiles)
            ]
            top = functools.reduce(jnp.maximum, x)
            total = None
            for c in range(tiles):
                e = jnp.exp2((x[c] - top) * scale_main)
                e_ref[slot, g * 8 : g * 8 + 8, c * LANES : (c + 1) * LANES] = e
                total = e if total is None else total + e
            tops.append(top)
            sums.append(total)
        tops = jnp.concatenate(tops, axis=0)
        sums = jnp.concatenate(sums, axis=0)
        f_ref[head, span] = tops
        row_top = jnp.max(tops, axis=1, keepdims=True)
        row_sum = jnp.sum(sums * jnp.exp2((tops - row_top) * scale_main), axis=1, keepdims=True)
        here = lax.broadcasted_iota(jnp.int32, (rows, LANES), 1) == head
        stm[span] = jnp.where(here, row_top, stm[span])
        stl[span] = jnp.where(here, row_sum, stl[span])

    def st_copy(st, i):
        return copy_to(st_tx.at[st], st_rx.at[st, i], st_s.at[st, i], st_r.at[st, i], ka_dev(i))

    def send_stats(st):
        st_tx[st, 0:heads] = jnp.transpose(stm[...], (1, 0))[0:heads]
        st_tx[st, heads : 2 * heads] = jnp.transpose(stl[...], (1, 0))[0:heads]
        for i in range(1, n_ka):
            st_copy(st, i).start()

    def finish(st):
        for i in range(1, n_ka):
            st_copy(st, i).wait_recv()
        tops = [st_tx[st, 0:heads]] + [st_rx[st, i, 0:heads] for i in range(1, n_ka)]
        sums = [st_tx[st, heads : 2 * heads]] + [st_rx[st, i, heads : 2 * heads] for i in range(1, n_ka)]
        top = functools.reduce(jnp.maximum, tops)
        total = functools.reduce(
            jnp.add, [b * jnp.exp2((a - top) * scale_main) for a, b in zip(tops, sums)]
        )
        comb[0:heads] = top
        comb[heads : 2 * heads] = 1.0 / (total * main_total)
        lo, hi = spans[st]
        rows = (hi - lo) * 32
        span = slice(lo * 32, hi * 32)
        cols = jnp.transpose(comb[...], (1, 0))[span]
        for head in range(heads):
            gtop = jnp.broadcast_to(cols[:, head : head + 1], (rows, LANES))
            ginv = jnp.broadcast_to(cols[:, heads + head : heads + head + 1], (rows, LANES))
            f_ref[head, span] = jnp.exp2((f_ref[head, span] - gtop) * scale_main) * ginv

        def one(g, carry):
            at = pl.ds(pl.multiple_of(g * 8, 8), 8)
            acc = [jnp.zeros((8, LANES), jnp.float32) for _ in range(tiles)]
            for head in range(heads):
                f = f_ref[head, pl.ds(pl.multiple_of(lo * 32 + g * 8, 8), 8), :]
                slot = eslot(st, head)
                for c in range(tiles):
                    acc[c] = acc[c] + f * e_ref[slot, at, c * LANES : (c + 1) * LANES]
            spot = lo + g // 4
            to = pl.ds(pl.multiple_of(lax.rem(g, 4) * 8, 8), 8)
            for c in range(tiles):
                part, inner = divmod(c, tiles // 2)
                t_ref[spot, part, to, inner * LANES : (inner + 1) * LANES] = acc[c]
            return carry

        lax.fori_loop(0, rows // 8, one, 0)

    def spot_of(offset):
        return offsets.index(offset)

    def ra_copy(a, c):
        src = t_ref.at[spot_of(half if a == 0 else -(half - a)), c]
        return copy_to(src, rxa.at[a, c], ra_s.at[a, c], ra_r.at[a, c], ha_dev(-1))

    def rb_copy(a, c):
        src = t_ref.at[spot_of(half - a), c]
        return copy_to(src, rxb.at[a, c], rb_s.at[a, c], rb_r.at[a, c], ha_dev(1))

    def chain_a(a, c):
        if a > 1 or (a == 1 and c == 0):
            ra_copy(a - 1, c).wait_recv()
            spot = spot_of(-(half - a))
            t_ref[spot, c] = t_ref[spot, c] + rxa[a - 1, c]
        ra_copy(a, c).start()

    def chain_b(a, c):
        if a > 1 or (a == 1 and c == 1):
            rb_copy(a - 1, c).wait_recv()
            spot = spot_of(half - a)
            t_ref[spot, c] = t_ref[spot, c] + rxb[a - 1, c]
        rb_copy(a, c).start()

    def fwd(st, after, early):
        last = st == len(spans) - 1
        kcopy(0, 0).wait()
        scores(st, 0, 0, s0)
        kcopy(NBUF, 0).start()

        def pair(i, carry):
            h0 = 2 * i
            a = lax.rem(h0 + 1, NBUF)
            b = lax.rem(h0 + 2, NBUF)
            kcopy(h0 + 1, a).wait()
            kcopy(h0 + 2, b).wait()
            scores(st, h0 + 1, a, s1)
            soften(st, h0, s0)
            scores(st, h0 + 2, b, s0)
            soften(st, h0 + 1, s1)

            def refill():
                kcopy(lax.rem(h0 + 1 + NBUF, heads), a).start()
                kcopy(lax.rem(h0 + 2 + NBUF, heads), b).start()

            if last:
                pl.when(h0 + 1 + NBUF < heads)(lambda: kcopy(h0 + 1 + NBUF, a).start())
                pl.when(h0 + 2 + NBUF < heads)(lambda: kcopy(h0 + 2 + NBUF, b).start())
            else:
                refill()
            after(i)
            return carry

        if early is None:
            lax.fori_loop(0, heads // 2 - 1, pair, 0)
        else:
            lax.fori_loop(0, 1, pair, 0)
            early()
            lax.fori_loop(1, heads // 2 - 1, pair, 0)
        end = (heads - 1) % NBUF
        kcopy(heads - 1, end).wait()
        scores(st, heads - 1, end, s1)
        if not last:
            kcopy(NBUF - 1, end).start()
        soften(st, heads - 2, s0)
        soften(st, heads - 1, s1)

    fwd(0, lambda i: None, greet)
    send_stats(0)

    def beside(i):
        @pl.when(i == EXTRA // 2 - 1)
        def _():
            finish(0)
            chain_a(0, 0)
            chain_b(0, 1)
            chain_a(1, 1)
            chain_b(1, 0)

    def beside_last(i):
        @pl.when(i == 1)
        def _():
            chain_a(1, 0)
            chain_b(1, 1)

        @pl.when(i == EXTRA // 2 - 1)
        def _():
            finish(1)

    fwd(1, beside, None)
    send_stats(1)
    fwd(2, beside_last, None)
    send_stats(2)

    iq_all[:, pl.ds(pl.multiple_of(h * 64, 64), 64), :] = iq_ref[:, pl.ds(pl.multiple_of(h * 64, 64), 64), :]
    wc_all[h] = wc_ref[h]
    ctx[pl.ds(pl.multiple_of(p * 256, 256), 256), :] = ik_ref[...]
    for i in range(1, n_pb):
        cx_copy(i).wait_recv()
    for i in range(1, n_ha):
        iq_copy(i).wait_recv()
        wc_copy(i).wait_recv()
    ctx_t[...] = jnp.transpose(ctx[...].astype(jnp.float32), (1, 0)).astype(jnp.bfloat16)
    for src in range(n_ha):
        for kk in range(n_ka // 2):
            spread = lane_spread(wc_all[src, kk : kk + 1, :])
            for one in range(2):
                w_rep[2 * kk + one, src * 64 : src * 64 + 64, :] = spread[one * 64 : one * 64 + 64]
        spread = lane_spread(wc_ref[src, pl.ds(k // 2, 1), :])
        w_own[src * 64 : src * 64 + 64, :] = jnp.where(lax.rem(k, 2) == 0, spread[0:64], spread[64:128])
    per = n_ha * 64
    for kk in range(n_ka):
        wq = jnp.transpose(w_rep[kk] * iq_all[kk].astype(jnp.float32), (1, 0))
        big = wq.astype(jnp.bfloat16)
        wq_t[0:128, kk * per : (kk + 1) * per] = big
        wq_t[128:256, kk * per : (kk + 1) * per] = (wq - big.astype(jnp.float32)).astype(jnp.bfloat16)

    step = 512

    def index_part(n, carry):
        kk, sc = n // (keys // step), lax.rem(n, keys // step)
        at = pl.ds(pl.multiple_of(sc * step, step), step)
        act = jnp.dot(iq_all[kk], ctx_t[:, at], preferred_element_type=jnp.float32)
        w = w_rep[kk]
        parts = []
        for c in range(step // LANES):
            a = act[:, c * LANES : (c + 1) * LANES]
            r = jnp.maximum(a, 0.0) * w
            parts.append(jnp.sum(jnp.sum(r.reshape(n_ha, 64, LANES), axis=0).reshape(8, 8, LANES), axis=1))
        lg[kk, :, at] = jnp.concatenate(parts, axis=1) * scale
        m_ref[kk, :, at] = jnp.where(act > 0, 1.0, 0.0).astype(jnp.bfloat16)
        return carry

    total_parts = n_ka * (keys // step)
    for c in (1, 0):
        chain_a(2, c)
        chain_b(2, 1 - c)
    lax.fori_loop(0, total_parts // 4, index_part, 0)
    finish(2)
    lax.fori_loop(total_parts // 4, total_parts, index_part, 0)
    for c in range(2):
        chain_a(3, c)
        chain_b(3, c)

    rel = pos_ref[n_ha - 1][:, 0:1] - first_key
    seen = lax.broadcasted_iota(jnp.int32, (32, keys), 1) <= rel
    logits = jnp.where(seen, lg[...].reshape(32, keys), LOW)
    row_top = jnp.max(logits, axis=1, keepdims=True)
    expo = jnp.where(seen, jnp.exp(logits - row_top), 0.0)
    row_sum = jnp.sum(expo, axis=1, keepdims=True)
    lg[...] = expo.reshape(n_ka, 8, keys)
    ix_tx[0] = jnp.broadcast_to(row_top, (32, LANES))
    ix_tx[1] = jnp.broadcast_to(row_sum, (32, LANES))

    def ix_copy(i):
        return copy_to(ix_tx, ix_rx.at[i], ix_s.at[i], ix_r.at[i], ka_dev(i))

    for i in range(1, n_ka):
        ix_copy(i).start()
    for i in range(1, n_ka):
        ix_copy(i).wait_recv()
    tops = [ix_tx[0]] + [ix_rx[i, 0] for i in range(1, n_ka)]
    sums = [ix_tx[1]] + [ix_rx[i, 1] for i in range(1, n_ka)]
    top = functools.reduce(jnp.maximum, tops)
    total = functools.reduce(jnp.add, [b * jnp.exp(a - top) for a, b in zip(tops, sums)])
    factor = (jnp.exp(tops[0] - top) / total)[:, 0:1]

    def diff_half(c):
        ra_copy(half - 1, c).wait_recv()
        rb_copy(half - 1, c).wait_recv()
        at = slice(c * (keys // 2), (c + 1) * (keys // 2))
        target = t_ref[n_ha - 1, c] + rxa[half - 1, c] + rxb[half - 1, c]
        diff = (lg[:, :, at].reshape(32, keys // 2) * factor - target) * (key_total / 16.0)
        big = diff.astype(jnp.bfloat16).astype(jnp.float32)
        small = diff - big
        for t in range(32):
            kk, r = divmod(t, 8)
            if r % 2:
                continue
            for value, ref in ((big, d_hi), (small, d_lo)):
                both = jnp.concatenate(
                    [
                        jnp.broadcast_to(value[t : t + 1], (8, keys // 2)),
                        jnp.broadcast_to(value[t + 1 : t + 2], (8, keys // 2)),
                    ],
                    axis=0,
                )
                ref[kk, r * 8 : r * 8 + 16, at] = both.astype(jnp.bfloat16)

    def gk_copy(i):
        return copy_to(gk_tx.at[i], gk_rx.at[i], gk_s.at[i], gk_r.at[i], pb_dev(i))

    def gated(kk, at, width, d_ref):
        return (m_ref[kk, :, at].reshape(n_ha, 64, width) * d_ref[kk, :, at][None]).reshape(per, width)

    def key_block(n, carry):
        dest = (n // many) * many + lax.rem(p + n, many)
        i = lax.rem(dest - p + n_pb, n_pb)
        at = pl.ds(pl.multiple_of(dest * 256, 256), 256)
        wide = jnp.zeros((256, 256), jnp.float32)
        thin = jnp.zeros((128, 256), jnp.float32)
        for kk in range(n_ka):
            hi = gated(kk, at, 256, d_hi)
            lo = gated(kk, at, 256, d_lo)
            wide += jnp.dot(wq_t[:, kk * per : (kk + 1) * per], hi, preferred_element_type=jnp.float32)
            thin += jnp.dot(wq_t[0:128, kk * per : (kk + 1) * per], lo, preferred_element_type=jnp.float32)
        block = (wide[0:128] + wide[128:256] + thin) * scale
        gk_tx[i] = jnp.transpose(block, (1, 0))

        @pl.when(i > 0)
        def _():
            gk_copy(i).start()

        return carry

    many = n_pb // 2
    for c in range(2):
        diff_half(c)
        lax.fori_loop(c * many, (c + 1) * many, key_block, 0)

    core, far = lax.rem(k, 2), k // 2

    def query_rows(part, kk):
        mask = jnp.concatenate(
            [m_ref[kk, src * 64 + part * 32 : src * 64 + part * 32 + 32, :] for src in range(n_ha)], axis=0
        ).reshape(n_ha, 32, keys)
        hi = (mask * d_hi[kk, part * 32 : part * 32 + 32, :][None]).reshape(n_ha * 32, keys)
        lo = (mask * d_lo[kk, part * 32 : part * 32 + 32, :][None]).reshape(n_ha * 32, keys)
        key = ctx[...]
        u_ref[part, kk] = jnp.dot(hi, key, preferred_element_type=jnp.float32) + jnp.dot(
            lo, key, preferred_element_type=jnp.float32
        )

    def u_copy(part, x):
        return copy_to(
            u_ref.at[part, x * 2 + 1 - core], u_rx.at[part, x], u_s.at[part, x], u_r.at[part, x],
            {"ka": far * 2 + 1 - core},
        )

    def v_copy(part):
        return copy_to(
            v_ref.at[part, 1 - far], v_rx.at[part], v_s.at[part], v_r.at[part], {"ka": (1 - far) * 2 + core}
        )

    def o_copy(part, i):
        dest = lax.rem(h + i, n_ha)
        return copy_to(
            r_ref.at[part, pl.ds(pl.multiple_of(dest * 32, 32), 32), :],
            o_rx.at[h, part * 32 : part * 32 + 32, :],
            o_s.at[part, i], o_r.at[part, i], ha_dev(i),
        )

    def z_copy(i):
        return copy_to(z_tx.at[lax.rem(h + i, n_ha)], z_rx.at[i], z_s.at[i], z_r.at[i], ha_dev(i))

    def y_copy(i):
        return copy_to(zsum.at[h], zsum.at[h], y_s.at[i], y_r.at[i], ha_dev(i))

    def other_core(part):
        for x in range(2):
            query_rows(part, x * 2 + 1 - core)
            u_copy(part, x).start()

    def own_core(part):
        for first in range(2):
            x = 1 - far if first == 0 else far
            query_rows(part, x * 2 + core)
            u_copy(part, x).wait_recv()
            v_ref[part, x] = u_ref[part, x * 2 + core] + u_rx[part, x]
            if first == 0:
                v_copy(part).start()

    def to_owners(part):
        v_copy(part).wait_recv()
        r_ref[part] = (v_ref[part, far] + v_rx[part]) * scale
        for i in range(1, n_ha):
            o_copy(part, i).start()
        o_rx[h, part * 32 : part * 32 + 32, :] = r_ref[part, pl.ds(pl.multiple_of(h * 32, 32), 32), :]

    other_core(0)
    own_core(0)
    other_core(1)
    to_owners(0)

    own = gk_tx[0]
    for i in range(1, n_pb):
        gk_copy(i).wait_recv()
        own = own + gk_rx[i]
    z_tx[...] = own.reshape(n_ha, 256 // n_ha, 128)
    for i in range(1, n_ha):
        z_copy(i).start()

    own_core(1)
    mine = z_tx[h]
    for i in range(1, n_ha):
        z_copy(i).wait_recv()
        mine = mine + z_rx[i]
    zsum[h] = mine
    for i in range(1, n_ha):
        y_copy(i).start()
    to_owners(1)

    for part in range(2):
        for i in range(1, n_ha):
            o_copy(part, i).wait_recv()
    weight_sums = jnp.zeros((8, 64), jnp.float32)
    for b in range(4):
        at = slice(b * LANES, (b + 1) * LANES)
        u = o_rx[2 * b : 2 * b + 2].reshape(LANES, 128)
        gq_ref[at, :] = u * w_own[at, :]
        dots = jnp.transpose(u * iq_ref[k, at, :].astype(jnp.float32), (1, 0))
        sums = jnp.broadcast_to(jnp.sum(dots, axis=0, keepdims=True), (8, LANES))
        sums = jnp.where(lax.rem(lane, 8) == lax.broadcasted_iota(jnp.int32, (8, LANES), 0), sums, 0.0)
        row = lax.broadcasted_iota(jnp.int32, (LANES, 64), 0) // 8 + b * (LANES // 8)
        pick = jnp.where(row == lax.broadcasted_iota(jnp.int32, (LANES, 64), 1), 1.0, 0.0)
        weight_sums = weight_sums + jnp.dot(
            sums, pick, precision=lax.Precision.HIGHEST, preferred_element_type=jnp.float32
        )
    gw_ref[...] = weight_sums

    for i in range(1, n_ha):
        y_copy(i).wait_recv()
    gk_ref[...] = zsum[...].reshape(256, 128)

    for i in range(1, n_pb):
        cx_copy(i).wait_send()
        gk_copy(i).wait_send()
    for i in range(1, n_ha):
        iq_copy(i).wait_send()
        wc_copy(i).wait_send()
        z_copy(i).wait_send()
        for part in range(2):
            o_copy(part, i).wait_send()
        y_copy(i).wait_send()
    for i in range(1, n_ka):
        for st in range(len(spans)):
            st_copy(st, i).wait_send()
        ix_copy(i).wait_send()
    for a in range(half):
        for c in range(2):
            if a or c == 0:
                ra_copy(a, c).wait_send()
            if a or c == 1:
                rb_copy(a, c).wait_send()
    for part in range(2):
        for x in range(2):
            u_copy(part, x).wait_send()
        v_copy(part).wait_send()


def hand_over(gq_in, gw_in, gk_in, gq_out, gw_out, gk_out):
    gq_out[...] = gq_in[...]
    gw_out[...] = gw_in[...]
    gk_out[...] = gk_in[...]


def body(sizes, main_query, main_key, index_query, index_weight, index_key, query_pos):
    n_pb, n_ha, n_ka = sizes
    t, heads, dh = main_query.shape
    keys = main_key.shape[0]
    joined = index_query.shape[1]
    dims = (n_pb, n_ha, n_ka, heads, dh, keys, heads * n_ha, keys * n_ka)
    qt = main_query.transpose(1, 2, 0)
    kt = main_key.transpose(1, 2, 0)
    iq = index_query.reshape(n_ka, n_ha * 64, 128)
    wc = index_weight.astype(jnp.float32).reshape(n_ka, n_ha, 64).transpose(1, 0, 2)
    wc = wc.reshape(n_ha, n_ka * 64 // LANES, LANES)
    pos = query_pos.astype(jnp.float32).reshape(n_ka, n_ha, 8).transpose(1, 0, 2).reshape(n_ha, 1, 32)
    pos = jnp.pad(pos, ((0, 0), (0, 7 - wc.shape[1]), (0, LANES - 32)))
    wc = jnp.concatenate([wc, pos], axis=1)

    half = n_ha // 2
    firsts, rows = stages(n_ha)
    n_st = len(firsts) - 1
    per = n_ha * 64
    f32, bf16 = jnp.float32, jnp.bfloat16
    scratch = [
        pltpu.VMEM((heads, t, dh), bf16),
        pltpu.VMEM((t, dh), f32),
        pltpu.VMEM((n_ha, 32, LANES), jnp.int32),
        pltpu.VMEM((per, LANES), f32),
        pltpu.VMEM((NBUF, dh, keys), bf16),
        pltpu.VMEM((rows, keys), f32),
        pltpu.VMEM((rows, keys), f32),
        pltpu.VMEM((heads + EXTRA, rows, keys), f32),
        pltpu.VMEM((heads, t, LANES), f32),
        pltpu.VMEM((t, LANES), f32),
        pltpu.VMEM((t, LANES), f32),
        pltpu.VMEM((n_st, 2 * heads, t), f32),
        pltpu.VMEM((n_st, n_ka, 2 * heads, t), f32),
        pltpu.VMEM((LANES, t), f32),
        pltpu.VMEM((n_ha, 2, 32, keys // 2), f32),
        pltpu.VMEM((half, 2, 32, keys // 2), f32),
        pltpu.VMEM((half, 2, 32, keys // 2), f32),
        pltpu.VMEM((n_ka, per, 128), bf16),
        pltpu.VMEM((n_ha, 8, LANES), f32),
        pltpu.VMEM((n_ka, per, LANES), f32),
        pltpu.VMEM((256, n_ka * per), bf16),
        pltpu.VMEM((keys, 128), bf16),
        pltpu.VMEM((128, keys), bf16),
        pltpu.VMEM((n_ka, per, keys), bf16),
        pltpu.VMEM((n_ka, 8, keys), f32),
        pltpu.VMEM((n_ka, 64, keys), bf16),
        pltpu.VMEM((n_ka, 64, keys), bf16),
        pltpu.VMEM((2, 32, LANES), f32),
        pltpu.VMEM((n_ka, 2, 32, LANES), f32),
        pltpu.VMEM((2, n_ka, per // 2, 128), f32),
        pltpu.VMEM((2, 2, per // 2, 128), f32),
        pltpu.VMEM((2, 2, per // 2, 128), f32),
        pltpu.VMEM((2, per // 2, 128), f32),
        pltpu.VMEM((2, per // 2, 128), f32),
        pltpu.VMEM((n_ha, 64, 128), f32),
        pltpu.VMEM((n_pb, 256, 128), f32),
        pltpu.VMEM((n_pb, 256, 128), f32),
        pltpu.VMEM((n_ha, 256 // n_ha, 128), f32),
        pltpu.VMEM((n_ha, 256 // n_ha, 128), f32),
        pltpu.VMEM((n_ha, 256 // n_ha, 128), f32),
    ]
    dma = pltpu.SemaphoreType.DMA
    sems = [dma((NBUF,))]
    for shape in (
        (n_st, n_ka), (half, 2), (half, 2), (n_ha,), (n_ha,), (n_pb,),
        (n_ka,), (2, 2), (2,), (2, n_ha), (n_pb,), (n_ha,), (n_ha,),
    ):
        sems += [dma(shape), dma(shape)]
    vmem = pl.BlockSpec(memory_space=pltpu.VMEM)
    gq, gw, gk = pl.pallas_call(
        functools.partial(kernel, dims),
        out_shape=(
            jax.ShapeDtypeStruct((per, 128), f32),
            jax.ShapeDtypeStruct((8, 64), f32),
            jax.ShapeDtypeStruct((256, 128), f32),
        ),
        in_specs=[vmem, pl.BlockSpec(memory_space=pl.ANY)] + [vmem] * 3,
        out_specs=(vmem, vmem, vmem),
        scratch_shapes=scratch + sems,
        compiler_params=pltpu.CompilerParams(
            collective_id=0, has_side_effects=True, vmem_limit_bytes=63 * 1024 * 1024
        ),
    )(qt, kt, iq, wc, index_key)
    gq, gw, gk = pl.pallas_call(
        hand_over,
        out_shape=tuple(jax.ShapeDtypeStruct(x.shape, f32) for x in (gq, gw, gk)),
        in_specs=[vmem] * 3,
        out_specs=(vmem,) * 3,
    )(gq, gw, gk)
    return (gq.reshape(t // n_ka, joined, 128), gw.T, gk)


def solution(mesh):
    placed = (
        P("pb", "ha", None),
        P("ka", "ha", None),
        P("pb", "ha", None),
        P("pb", "ha"),
        P(("pb", "ka"), None),
        P("pb"),
    )
    sizes = tuple(mesh.shape[name] for name in ("pb", "ha", "ka"))
    return jax.shard_map(
        functools.partial(body, sizes),
        mesh=mesh,
        in_specs=placed,
        out_specs=(P(("pb", "ka"), "ha", None), P(("pb", "ka"), "ha"), P(("pb", "ka"), None)),
        check_vma=False,
    )
```
